32 devices in a mesh: sec: 4 (over y, x), col: 8 (over z, core).
Axes of the slice: x: 2, y: 2, z: 4, core: 2. Of those that a mesh axis runs over, the one named last changes fastest.
Arguments:
- column_state: float32 [4, 40960, 128], P('sec', 'col'), may hold values from -6 to 6
- mixing: float32 [4, 40960, 128], P('sec', 'col'), may hold values from 0.05 to 20
- surface_mask: int32 [4, 64, 128], P('sec', 'col'), may hold values 0 or 1
- pairings: int32 [4, 432, 3], P('sec', 'col'), may hold values from 0 to 255, as said below
- pairing_count: int32 [4, 8], P('sec', 'col'), may hold values from 3 to 54, as said below
- remap_weights: float32 [4, 16384, 128], P('sec', 'col'), may hold values from -0.5 to 0.5
Outputs:
- new_state: float32 [4, 40960, 128], P('sec', 'col')
The draws below stay inside these ranges and needn't reach their ends.
Inputs may be any that keep to these rules, and one draw needn't show every extreme that they name: `pairings`: entry e of device d's list is used when e < pairing_count of d; used entries come first. Column 0 is a block of d, column 2 a weight block of d (below 16), column 1 a global block of the other component (ocean blocks for atmosphere devices, atmosphere blocks for ocean devices) on a device whose col differs from d's by -1, 0 or 1 cyclically. At most 6 used entries of one device name blocks of any one device. `pairing_count`: atmosphere devices use at most 18 entries.
All inputs are finite; a program needn't handle non-finite values. No bound on the sum of `surface_mask` on one device may be relied on, other than what follows from the above.
Results may differ from the reference program's by a relative error of at most 0.0003.
Values sent between devices are 32-bit elements; how exact they have to be, the bound alone decides.
A program may use at most 192 MiB of HBM per device.

```python
import math
import jax
import jax.numpy as jnp
from jax import lax

CELLS = 128
LEV_ATM = 128
LEV_OCN = 80
TRC_ATM = 5
TRC_OCN = 8
COUPLED = 4
BLK_DEV = 8
CAP = 6
WBLK = 16
SUBSTEPS = 2
OVL = 54
ROWS_DEV = 5120
NBLK = 256
N_SEC = 4
N_COL = 8


def pairing_tables(key):
    device_total = N_SEC * N_COL
    pair_total = 3 * (N_SEC - 1)
    slot_total = pair_total * CAP
    device_ids = jnp.arange(device_total, dtype=jnp.int32)
    device_sec = device_ids // N_COL
    device_col = device_ids % N_COL
    ocean_rows = device_sec == N_SEC - 1
    pair_index = jnp.arange(pair_total, dtype=jnp.int32)
    col_shift = pair_index % 3 - 1
    peer_col = (device_col[:, None] + col_shift[None, :]) % N_COL
    peer_sec = jnp.where(ocean_rows[:, None], pair_index[None, :] // 3, N_SEC - 1)
    allowed = ocean_rows[:, None] | (pair_index[None, :] < 3)
    focus_col = jax.random.randint(jax.random.fold_in(key, 11), (), 0, N_COL)
    pair_sizes = jax.random.randint(jax.random.fold_in(key, 12), (device_total, pair_total), 1, CAP + 1)
    forced = (device_col[:, None] == focus_col) | (peer_col == focus_col)
    pair_sizes = jnp.where(forced, CAP, pair_sizes)
    pair_sizes = jnp.where(allowed, pair_sizes, 0)
    slot_index = jnp.arange(slot_total, dtype=jnp.int32)
    slot_pair = slot_index // CAP
    slot_rank = slot_index % CAP
    in_use = slot_rank[None, :] < pair_sizes[:, slot_pair]
    scores = jax.random.randint(jax.random.fold_in(key, 13), (device_total, slot_total), 0, 65536)
    scores = jnp.where(in_use, scores, scores + 65536) * slot_total + slot_index[None, :]
    ordering = jnp.argsort(scores, axis=1).astype(jnp.int32)
    entry_pair = ordering // CAP
    target_sec = jnp.take_along_axis(peer_sec, entry_pair, axis=1)
    target_col = jnp.take_along_axis(peer_col, entry_pair, axis=1)
    local_block = jax.random.randint(jax.random.fold_in(key, 14), (device_total, slot_total), 0, BLK_DEV)
    target_block = (target_sec * N_COL + target_col) * BLK_DEV + local_block
    source_block = jax.random.randint(jax.random.fold_in(key, 15), (device_total, slot_total), 0, BLK_DEV)
    weight_block = jax.random.randint(jax.random.fold_in(key, 16), (device_total, slot_total), 0, WBLK)
    listing = jnp.stack([source_block, target_block, weight_block], axis=-1).astype(jnp.int32)
    totals = jnp.sum(pair_sizes, axis=1).astype(jnp.int32)
    return (listing.reshape(N_SEC, N_COL * slot_total, 3), totals.reshape(N_SEC, N_COL))


def draw_pairings(key, part):
    return pairing_tables(key)[0]


def draw_pairing_count(key, part):
    return pairing_tables(key)[1]


def with_ends(result, own_key, smallest, high):
    longest = result.shape.index(max(result.shape))
    spots = []
    for shift in (0, 1):
        where = [jax.random.randint(jax.random.fold_in(own_key, axis), (), 0, length) for axis, length in enumerate(result.shape)]
        where[longest] = (where[longest] + shift) % result.shape[longest]
        spots.append(tuple(where))
    return result.at[spots[0]].set(smallest).at[spots[1]].set(high)


def shard_levels(own_key, extent, pieces, low, largest):
    level, own = 1.0, jax.random.fold_in(own_key, 6)
    for position, parts in pieces:
        draws = jnp.exp(jax.random.uniform(jax.random.fold_in(own, position), (parts,), jnp.float32, low / len(pieces), largest / len(pieces)))
        level = level * jnp.repeat(draws, extent[position] // parts).reshape([-1 if axis == position else 1 for axis in range(len(extent))])
    return level


def normal_values(key, dims, scale, most, pieces=(), kind=jnp.bfloat16):
    gain = shard_levels(key, dims, pieces, -0.22, 0.18) if pieces else 1.0
    array = jax.random.normal(key, dims, jnp.float32) * scale * gain
    return jnp.minimum(jnp.maximum(array, -most), most).astype(kind)


def setup_inputs(seed: int = 0) -> dict:
    streams_of = jax.random.split(jax.random.key(seed), 7)
    column_state = normal_values(streams_of[0], (N_SEC, N_COL * ROWS_DEV, CELLS), 1.0, 6.0, ((0, 4), (1, 8)), jnp.float32)
    mixing = jnp.clip(jnp.exp(math.log(20.0) - 5.9914645 * jax.random.uniform(streams_of[1], (N_SEC, N_COL * ROWS_DEV, CELLS), jnp.float32) ** shard_levels(streams_of[1], (N_SEC, N_COL * ROWS_DEV, CELLS), ((0, 4), (1, 8)), -0.2, 0.2)), 0.05, 20.0)
    surface_mask = with_ends((jax.random.randint(streams_of[2], (N_SEC, N_COL * BLK_DEV, CELLS), 0, 4) < 3).astype(jnp.int32), jax.random.fold_in(streams_of[2], 1), 0, 1)
    pairings = draw_pairings(jax.random.fold_in(streams_of[6], 71), 0)
    pairing_count = draw_pairing_count(jax.random.fold_in(streams_of[6], 71), 0)
    remap_weights = normal_values(streams_of[5], (N_SEC, N_COL * WBLK * CELLS, CELLS), CELLS ** -0.5, 0.5, ((0, 4), (1, 8)), jnp.float32)
    return dict(column_state=column_state, mixing=mixing, surface_mask=surface_mask, pairings=pairings, pairing_count=pairing_count, remap_weights=remap_weights)


highest = lax.Precision.HIGHEST


def tridiagonal(right_side, coupling, interface):
    shifted = jnp.concatenate([jnp.zeros_like(coupling[:1]), coupling[:-1]], axis=0)
    diagonal = 1.0 + shifted + coupling
    deepest = right_side.shape[0] - 1
    right_side = right_side.at[deepest].add(coupling[deepest] * interface)

    def forward(carried, inputs):
        upper_prev, solved_prev = carried
        lower_band, diag_band, upper_band, source = inputs
        divisor = diag_band - lower_band * upper_prev
        upper_next = upper_band / divisor
        solved_next = (source - lower_band * solved_prev) / divisor
        return (upper_next, solved_next), (upper_next, solved_next)

    initial = (jnp.zeros_like(interface), jnp.zeros_like(interface))
    _, (uppers, partial_values) = lax.scan(forward, initial, (-shifted, diagonal, -coupling, right_side))

    def backward(following, inputs):
        upper_band, partial_value = inputs
        current = partial_value - upper_band * following
        return current, current

    _, solved = lax.scan(backward, jnp.zeros_like(interface), (uppers, partial_values), reverse=True)
    return solved


def remap(values, listing, used_count, weights):
    def one_device(operands):
        surface_vals, table_rows, count_here, weight_rows = operands
        entries = jnp.einsum('enc,ecd->end', surface_vals[table_rows[:, 0]], weight_rows[table_rows[:, 2]], precision=highest)
        in_use = jnp.arange(OVL, dtype=jnp.int32) < count_here
        target = jnp.where(in_use, table_rows[:, 1], NBLK).astype(jnp.int32)
        return entries, target

    entries, target = lax.map(one_device, (values, listing, used_count, weights))
    summed = jnp.zeros((NBLK, COUPLED, CELLS), jnp.float32)
    return summed.at[target.reshape(-1)].add(entries.reshape(-1, COUPLED, CELLS), mode="drop")


def reference(column_state, mixing, surface_mask, pairings, pairing_count, remap_weights):
    devices_all = N_SEC * N_COL
    listing = pairings.reshape(devices_all, OVL, 3)
    used_count = pairing_count.reshape(devices_all)
    weights = remap_weights.reshape(devices_all, WBLK, CELLS, CELLS)
    surface = surface_mask.astype(jnp.float32).reshape(N_SEC, N_COL, BLK_DEV, CELLS)
    shapes = [(LEV_ATM, TRC_ATM) if section < N_SEC - 1 else (LEV_OCN, TRC_OCN) for section in range(N_SEC)]
    profiles = []
    couplings = []
    for section in range(N_SEC):
        levels, tracers = shapes[section]
        profile = column_state[section].reshape(N_COL, levels, BLK_DEV, tracers, CELLS)
        coupling = mixing[section].reshape(N_COL, levels, BLK_DEV, tracers, CELLS)
        coupling = coupling.at[:, levels - 1].multiply(surface[section][:, :, None, :])
        profiles.append(jnp.moveaxis(profile, 1, 0).reshape(levels, N_COL * BLK_DEV * tracers, CELLS))
        couplings.append(jnp.moveaxis(coupling, 1, 0).reshape(levels, N_COL * BLK_DEV * tracers, CELLS))
    for substep in range(SUBSTEPS):
        values = []
        for section in range(N_SEC):
            levels, tracers = shapes[section]
            bottom = profiles[section][levels - 1].reshape(N_COL, BLK_DEV, tracers, CELLS)[:, :, :COUPLED]
            values.append(bottom * surface[section][:, :, None, :])
        values = jnp.stack(values).reshape(devices_all, BLK_DEV, COUPLED, CELLS)
        boundary = remap(values, listing, used_count, weights).reshape(N_SEC, N_COL, BLK_DEV, COUPLED, CELLS)
        for section in range(N_SEC):
            levels, tracers = shapes[section]
            padding = jnp.zeros((N_COL, BLK_DEV, tracers - COUPLED, CELLS), jnp.float32)
            interface = jnp.concatenate([boundary[section], padding], axis=2).reshape(-1, CELLS)
            profiles[section] = tridiagonal(profiles[section], couplings[section], interface)
    outputs = []
    for section in range(N_SEC):
        levels, tracers = shapes[section]
        restored = jnp.moveaxis(profiles[section].reshape(levels, N_COL, BLK_DEV, tracers, CELLS), 0, 1)
        outputs.append(restored.reshape(N_COL * levels * BLK_DEV * tracers, CELLS))
    return jnp.stack(outputs)
```

```python
from functools import partial

import jax
import jax.numpy as jnp
from jax import lax
from jax.experimental import pallas as pl
from jax.experimental.pallas import tpu as pltpu
from jax.sharding import PartitionSpec as P

LEV_ATM = 128
LEV_OCN = 80
TRC_ATM = 5
TRC_OCN = 8
COUPLED = 4
SEGMENT = 16

MESH = pl.DeviceIdType.MESH


def split(values):
    high = values.astype(jnp.bfloat16)
    low = (values - high.astype(jnp.float32)).astype(jnp.bfloat16)
    return high, low


def reciprocal(values):
    first = pl.reciprocal(values, approx=True)
    return first * (2.0 - values * first)


def kernel(sections, columns, blocks, kinds, cells, state_hbm, mixing_hbm, mask_hbm, pairs_hbm, count_ref, weights_hbm,
           out_hbm, state, rate, inverse, solved, weights, split_weights, mask, pairs, last, edge, send, recv,
           in_sem, chunk_sem, out_sem, send_sem, recv_sem):
    section = lax.axis_index("sec")
    column = lax.axis_index("col")
    is_ocean = section == sections - 1

    def wrapped(index):
        return lax.rem(index + columns, columns)

    def program(levels, tracers, peers, chunk_segments):
        rows = blocks * tracers
        deepest = (levels - 1) * rows
        chunk = chunk_segments * SEGMENT * rows
        chunks = levels // (chunk_segments * SEGMENT)

        barrier = pltpu.get_barrier_semaphore()
        for peer_sec, peer_col, _ in peers:
            pl.semaphore_signal(barrier, inc=1, device_id=(peer_sec, peer_col), device_id_type=MESH)

        mask_copy = pltpu.make_async_copy(mask_hbm.at[0], mask, in_sem.at[0])
        pairs_copy = pltpu.make_async_copy(pairs_hbm, pairs, in_sem.at[1])
        last_copy = pltpu.make_async_copy(
            state_hbm.at[0, pl.ds(deepest, rows)], last.at[pl.ds(0, rows)], in_sem.at[2])
        weights_copy = pltpu.make_async_copy(weights_hbm.at[0], weights, in_sem.at[3])
        first_copies = (mask_copy, pairs_copy, last_copy, weights_copy)
        for copy in first_copies:
            copy.start()
        chunk_copies = []
        for index in range(chunks):
            span = pl.ds(index * chunk, chunk)
            chunk_copies.append((
                pltpu.make_async_copy(mixing_hbm.at[0, span], rate.at[span], chunk_sem.at[0, index]),
                pltpu.make_async_copy(state_hbm.at[0, span], state.at[span], chunk_sem.at[1, index]),
            ))
        for pair in chunk_copies:
            for copy in pair:
                copy.start()

        mask_copy.wait()
        pairs_copy.wait()
        list_length = pairs.shape[2]
        count_rows = -(-len(peers) * blocks // 16) * 16
        row = lax.broadcasted_iota(jnp.int32, (count_rows, 1), 0)
        wanted = jnp.full((count_rows, 1), -1, jnp.int32)
        for index, (peer_sec, peer_col, _) in enumerate(peers):
            first = (peer_sec * columns + peer_col) * blocks - index * blocks
            wanted = jnp.where((row >= index * blocks) & (row < (index + 1) * blocks), first + row, wanted)
        position = lax.broadcasted_iota(jnp.int32, (1, list_length), 1)
        target = jnp.where(position < count_ref[0, 0], pairs[1], -2)
        product = pairs[2] * blocks + pairs[0]
        to_rows = (target == wanted).astype(jnp.bfloat16)
        from_rows = (product == lax.broadcasted_iota(jnp.int32, (kinds * blocks, 1), 0)).astype(jnp.bfloat16)
        counts = lax.dot_general(
            to_rows, from_rows, (((1,), (1,)), ((), ())), preferred_element_type=jnp.float32).astype(jnp.bfloat16)
        counts_twice = jnp.concatenate([counts, counts], axis=1)
        sea = mask[...].astype(jnp.float32)

        edge[...] = jnp.zeros_like(edge)
        for field in range(tracers):
            edge[pl.ds(field, blocks, stride=tracers), :] = sea
        open_sea = edge[pl.ds(0, rows), :]
        edge[...] = jnp.zeros_like(edge)

        def exchange(step):
            surface = jnp.concatenate(
                [last[pl.ds(field, blocks, stride=tracers), :] * sea for field in range(COUPLED)], axis=0)
            surface_split = jnp.concatenate(split(surface), axis=0)
            half = COUPLED * blocks
            products = []
            for kind in range(kinds):
                span = pl.ds(kind * cells, cells)
                if step == 0:
                    both = jnp.concatenate(split(weights[span, :]), axis=1)
                    split_weights[span, :] = both
                else:
                    both = split_weights[span, :]
                parts = jnp.dot(surface_split, both, preferred_element_type=jnp.float32)
                products.append(
                    (parts[:half, :cells] + parts[half:, :cells]) + (parts[:half, cells:] + parts[half:, cells:]))
            ordered = jnp.concatenate(
                [jnp.concatenate([item[field * blocks:(field + 1) * blocks] for item in products], axis=0)
                 for field in range(COUPLED)], axis=1)
            outgoing = jnp.dot(
                counts_twice, jnp.concatenate(split(ordered), axis=0), preferred_element_type=jnp.float32)
            copies = []
            for index, (peer_sec, peer_col, slot) in enumerate(peers):
                send[step, index] = outgoing[index * blocks:(index + 1) * blocks]
            if step == 0:
                pl.semaphore_wait(barrier, len(peers))
            for index, (peer_sec, peer_col, slot) in enumerate(peers):
                copy = pltpu.make_async_remote_copy(
                    src_ref=send.at[step, index], dst_ref=recv.at[step, slot],
                    send_sem=send_sem.at[step, index], recv_sem=recv_sem.at[step, slot],
                    device_id=(peer_sec, peer_col), device_id_type=MESH)
                copy.start()
                copies.append(copy)
            return copies

        def arrived(step):
            total = None
            for index, (peer_sec, peer_col, _) in enumerate(peers):
                pltpu.make_async_remote_copy(
                    src_ref=send.at[step, index], dst_ref=recv.at[step, index],
                    send_sem=send_sem.at[step, index], recv_sem=recv_sem.at[step, index],
                    device_id=(peer_sec, peer_col), device_id_type=MESH).wait_recv()
            for index in range(len(peers)):
                part = recv[step, index]
                total = part if total is None else total + part
            for field in range(COUPLED):
                edge[pl.ds(field, blocks, stride=tracers), :] = total[:, field * cells:(field + 1) * cells]
            return edge[pl.ds(0, rows), :]

        def at(level):
            return pl.ds(pl.multiple_of(level * rows, 8), rows)

        def factor(segment, carried):
            numer, value, above = carried
            denom = jnp.ones_like(numer)
            for offset in range(SEGMENT):
                here = at(segment * SEGMENT + offset)
                coupling = rate[here, :]
                next_denom = numer + coupling * denom
                numer = next_denom + coupling * numer
                scale = denom * reciprocal(next_denom)
                value = scale * state[here, :] + (scale * above) * value
                inverse[here, :] = scale
                solved[here, :] = value
                denom = next_denom
                above = coupling
            return numer * reciprocal(denom), value, above

        def back_first(index, below):
            segment = levels // SEGMENT - 1 - index
            for offset in reversed(range(SEGMENT)):
                here = at(segment * SEGMENT + offset)
                below = solved[here, :] + (inverse[here, :] * rate[here, :]) * below
                solved[here, :] = below
            return below

        def forward_second(segment, carried):
            value, above = carried
            for offset in range(SEGMENT):
                here = at(segment * SEGMENT + offset)
                scale = inverse[here, :]
                coupling = rate[here, :]
                value = scale * solved[here, :] + (scale * above) * value
                solved[here, :] = value
                inverse[here, :] = scale * coupling
                above = coupling
            return value, above

        def back_second(index, below):
            segment = levels // SEGMENT - 1 - index
            for offset in reversed(range(SEGMENT)):
                here = at(segment * SEGMENT + offset)
                below = solved[here, :] + inverse[here, :] * below
                state[here, :] = below
            return below

        last_copy.wait()
        weights_copy.wait()
        sends = exchange(0)

        zeros = jnp.zeros((rows, cells), jnp.float32)
        carried = (jnp.ones_like(zeros), zeros, zeros)
        for index, pair in enumerate(chunk_copies):
            for copy in pair:
                copy.wait()
            if index == chunks - 1:
                rate[pl.ds(deepest, rows), :] = rate[pl.ds(deepest, rows), :] * open_sea
            carried = lax.fori_loop(index * chunk_segments, (index + 1) * chunk_segments, factor, carried)

        boundary = arrived(0)
        bottom = pl.ds(deepest, rows)
        last[pl.ds(0, rows), :] = solved[bottom, :] + (inverse[bottom, :] * rate[bottom, :]) * boundary
        sends += exchange(1)
        lax.fori_loop(0, levels // SEGMENT, back_first, boundary)
        lax.fori_loop(0, levels // SEGMENT, forward_second, (zeros, zeros))
        below = arrived(1)
        out_copies = []
        for index in reversed(range(chunks)):
            done = (chunks - 1 - index) * chunk_segments
            below = lax.fori_loop(done, done + chunk_segments, back_second, below)
            span = pl.ds(index * chunk, chunk)
            copy = pltpu.make_async_copy(state.at[span], out_hbm.at[0, span], out_sem.at[index])
            copy.start()
            out_copies.append(copy)
        for copy in sends:
            copy.wait_send()
        for copy in out_copies:
            copy.wait()

    @pl.when(is_ocean)
    def _():
        peers = [(sec, wrapped(column + shift - 1), 2 - shift) for sec in range(sections - 1) for shift in range(3)]
        program(LEV_OCN, TRC_OCN, peers, 1)

    @pl.when(jnp.logical_not(is_ocean))
    def _():
        peers = [(sections - 1, wrapped(column + shift - 1), section * 3 + 2 - shift) for shift in range(3)]
        program(LEV_ATM, TRC_ATM, peers, 2)


def shards(column_state, mixing, surface_mask, pairings, pairing_count, remap_weights):
    sections = lax.axis_size("sec")
    columns = lax.axis_size("col")
    _, rows_all, cells = column_state.shape
    blocks = surface_mask.shape[1]
    weight_rows = remap_weights.shape[1]
    kinds = weight_rows // cells
    rows_most = blocks * max(TRC_ATM, TRC_OCN)
    peers_most = 3 * (sections - 1)
    chunks_most = 5
    listing = jnp.transpose(pairings, (2, 0, 1))
    anywhere = pl.BlockSpec(memory_space=pl.ANY)
    column_buffer = pltpu.VMEM((rows_all, cells), jnp.float32)
    return pl.pallas_call(
        partial(kernel, sections, columns, blocks, kinds, cells),
        out_shape=jax.ShapeDtypeStruct(column_state.shape, jnp.float32),
        in_specs=[anywhere, anywhere, anywhere, anywhere, pl.BlockSpec(memory_space=pltpu.SMEM), anywhere],
        out_specs=anywhere,
        scratch_shapes=[
            column_buffer, column_buffer, column_buffer, column_buffer,
            pltpu.VMEM((weight_rows, cells), jnp.float32),
            pltpu.VMEM((weight_rows, 2 * cells), jnp.bfloat16),
            pltpu.VMEM((blocks, cells), jnp.int32),
            pltpu.VMEM(listing.shape, jnp.int32),
            pltpu.VMEM((rows_most, cells), jnp.float32),
            pltpu.VMEM((rows_most, cells), jnp.float32),
            pltpu.VMEM((2, peers_most, blocks, COUPLED * cells), jnp.float32),
            pltpu.VMEM((2, peers_most, blocks, COUPLED * cells), jnp.float32),
            pltpu.SemaphoreType.DMA((4,)),
            pltpu.SemaphoreType.DMA((2, chunks_most)),
            pltpu.SemaphoreType.DMA((chunks_most,)),
            pltpu.SemaphoreType.DMA((2, peers_most)),
            pltpu.SemaphoreType.DMA((2, peers_most)),
        ],
        compiler_params=pltpu.CompilerParams(
            collective_id=0, has_side_effects=True, vmem_limit_bytes=40 * 1024 * 1024),
    )(column_state, mixing, surface_mask, listing, pairing_count, remap_weights)


def solution(mesh):
    placed = (
        P("sec", "col", None),
        P("sec", "col", None),
        P("sec", "col", None),
        P("sec", "col", None),
        P("sec", "col"),
        P("sec", "col", None),
    )
    return jax.shard_map(
        shards, mesh=mesh, in_specs=placed, out_specs=P("sec", "col", None), check_vma=False
    )
```

```python
from functools import partial

import jax
import jax.numpy as jnp
from jax import lax
from jax.experimental import pallas as pl
from jax.experimental.pallas import tpu as pltpu
from jax.sharding import PartitionSpec as P

LEV_ATM = 128
LEV_OCN = 80
TRC_ATM = 5
TRC_OCN = 8
COUPLED = 4
SEGMENT = 16
WEIGHT_PARTS = 4

MESH = pl.DeviceIdType.MESH


def split(values):
    high = values.astype(jnp.bfloat16)
    low = (values - high.astype(jnp.float32)).astype(jnp.bfloat16)
    return high, low


def reciprocal(values):
    first = pl.reciprocal(values, approx=True)
    return first * (2.0 - values * first)


def kernel(sections, columns, blocks, kinds, cells, state_hbm, mixing_hbm, mask_hbm, pairs_hbm, count_ref, weights_hbm,
           out_hbm, state, rate, inverse, solved, weights, split_weights, mask, pairs, last, edge, send, recv,
           in_sem, chunk_sem, out_sem, send_sem, recv_sem):
    section = lax.axis_index("sec")
    column = lax.axis_index("col")
    is_ocean = section == sections - 1

    def wrapped(index):
        return lax.rem(index + columns, columns)

    def program(levels, tracers, peers, chunk_segments):
        rows = blocks * tracers
        deepest = (levels - 1) * rows
        chunk = chunk_segments * SEGMENT * rows
        chunks = levels // (chunk_segments * SEGMENT)

        barrier = pltpu.get_barrier_semaphore()
        for peer_sec, peer_col, _ in peers:
            pl.semaphore_signal(barrier, inc=1, device_id=(peer_sec, peer_col), device_id_type=MESH)

        mask_copy = pltpu.make_async_copy(mask_hbm.at[0], mask, in_sem.at[0])
        pairs_copy = pltpu.make_async_copy(pairs_hbm, pairs, in_sem.at[1])
        last_copy = pltpu.make_async_copy(
            state_hbm.at[0, pl.ds(deepest, rows)], last.at[pl.ds(0, rows)], in_sem.at[2])
        part = weights.shape[0] // WEIGHT_PARTS
        weights_copies = [
            pltpu.make_async_copy(
                weights_hbm.at[0, pl.ds(index * part, part)], weights.at[pl.ds(index * part, part)], in_sem.at[3 + index])
            for index in range(WEIGHT_PARTS)]
        first_copies = (mask_copy, pairs_copy, last_copy, *weights_copies)
        for copy in first_copies:
            copy.start()
        chunk_copies = []
        for index in range(chunks):
            span = pl.ds(index * chunk, chunk)
            chunk_copies.append((
                pltpu.make_async_copy(mixing_hbm.at[0, span], rate.at[span], chunk_sem.at[0, index]),
                pltpu.make_async_copy(state_hbm.at[0, span], state.at[span], chunk_sem.at[1, index]),
            ))
        for pair in chunk_copies:
            for copy in pair:
                copy.start()

        mask_copy.wait()
        pairs_copy.wait()
        list_length = pairs.shape[2]
        count_rows = -(-len(peers) * blocks // 16) * 16
        row = lax.broadcasted_iota(jnp.int32, (count_rows, 1), 0)
        wanted = jnp.full((count_rows, 1), -1, jnp.int32)
        for index, (peer_sec, peer_col, _) in enumerate(peers):
            first = (peer_sec * columns + peer_col) * blocks - index * blocks
            wanted = jnp.where((row >= index * blocks) & (row < (index + 1) * blocks), first + row, wanted)
        position = lax.broadcasted_iota(jnp.int32, (1, list_length), 1)
        target = jnp.where(position < count_ref[0, 0], pairs[1], -2)
        product = pairs[2] * blocks + pairs[0]
        to_rows = (target == wanted).astype(jnp.bfloat16)
        from_rows = (product == lax.broadcasted_iota(jnp.int32, (kinds * blocks, 1), 0)).astype(jnp.bfloat16)
        counts = lax.dot_general(
            to_rows, from_rows, (((1,), (1,)), ((), ())), preferred_element_type=jnp.float32).astype(jnp.bfloat16)
        counts_twice = jnp.concatenate([counts, counts], axis=1)
        sea = mask[...].astype(jnp.float32)

        edge[...] = jnp.zeros_like(edge)
        for field in range(tracers):
            edge[pl.ds(field, blocks, stride=tracers), :] = sea
        open_sea = edge[pl.ds(0, rows), :]
        edge[...] = jnp.zeros_like(edge)

        def exchange(step):
            surface = jnp.concatenate(
                [last[pl.ds(field, blocks, stride=tracers), :] * sea for field in range(COUPLED)], axis=0)
            surface_split = jnp.concatenate(split(surface), axis=0)
            half = COUPLED * blocks
            products = []
            for kind in range(kinds):
                span = pl.ds(kind * cells, cells)
                if step == 0:
                    both = jnp.concatenate(split(weights[span, :]), axis=1)
                    split_weights[span, :] = both
                else:
                    both = split_weights[span, :]
                parts = jnp.dot(surface_split, both, preferred_element_type=jnp.float32)
                products.append(
                    (parts[:half, :cells] + parts[half:, :cells]) + (parts[:half, cells:] + parts[half:, cells:]))
            ordered = jnp.concatenate(
                [jnp.concatenate([item[field * blocks:(field + 1) * blocks] for item in products], axis=0)
                 for field in range(COUPLED)], axis=1)
            outgoing = jnp.dot(
                counts_twice, jnp.concatenate(split(ordered), axis=0), preferred_element_type=jnp.float32)
            copies = []
            for index, (peer_sec, peer_col, slot) in enumerate(peers):
                send[step, index] = outgoing[index * blocks:(index + 1) * blocks]
            if step == 0:
                pl.semaphore_wait(barrier, len(peers))
            for index, (peer_sec, peer_col, slot) in enumerate(peers):
                copy = pltpu.make_async_remote_copy(
                    src_ref=send.at[step, index], dst_ref=recv.at[step, slot],
                    send_sem=send_sem.at[step, index], recv_sem=recv_sem.at[step, slot],
                    device_id=(peer_sec, peer_col), device_id_type=MESH)
                copy.start()
                copies.append(copy)
            return copies

        def arrived(step):
            total = None
            for index, (peer_sec, peer_col, _) in enumerate(peers):
                pltpu.make_async_remote_copy(
                    src_ref=send.at[step, index], dst_ref=recv.at[step, index],
                    send_sem=send_sem.at[step, index], recv_sem=recv_sem.at[step, index],
                    device_id=(peer_sec, peer_col), device_id_type=MESH).wait_recv()
            for index in range(len(peers)):
                part = recv[step, index]
                total = part if total is None else total + part
            for field in range(COUPLED):
                edge[pl.ds(field, blocks, stride=tracers), :] = total[:, field * cells:(field + 1) * cells]
            return edge[pl.ds(0, rows), :]

        def at(level):
            return pl.ds(pl.multiple_of(level * rows, 8), rows)

        def factor(segment, carried):
            numer, value, above = carried
            denom = jnp.ones_like(numer)
            for offset in range(SEGMENT):
                here = at(segment * SEGMENT + offset)
                coupling = rate[here, :]
                next_denom = numer + coupling * denom
                numer = next_denom + coupling * numer
                scale = denom * reciprocal(next_denom)
                value = scale * state[here, :] + (scale * above) * value
                inverse[here, :] = scale
                solved[here, :] = value
                denom = next_denom
                above = coupling
            return numer * reciprocal(denom), value, above

        def back_first(index, below):
            segment = levels // SEGMENT - 1 - index
            for offset in reversed(range(SEGMENT)):
                here = at(segment * SEGMENT + offset)
                below = solved[here, :] + (inverse[here, :] * rate[here, :]) * below
                solved[here, :] = below
            return below

        def forward_second(segment, carried):
            value, above = carried
            for offset in range(SEGMENT):
                here = at(segment * SEGMENT + offset)
                scale = inverse[here, :]
                coupling = rate[here, :]
                value = scale * solved[here, :] + (scale * above) * value
                solved[here, :] = value
                inverse[here, :] = scale * coupling
                above = coupling
            return value, above

        def back_second(index, below):
            segment = levels // SEGMENT - 1 - index
            for offset in reversed(range(SEGMENT)):
                here = at(segment * SEGMENT + offset)
                below = solved[here, :] + inverse[here, :] * below
                state[here, :] = below
            return below

        last_copy.wait()
        for copy in weights_copies:
            copy.wait()
        sends = exchange(0)

        zeros = jnp.zeros((rows, cells), jnp.float32)
        carried = (jnp.ones_like(zeros), zeros, zeros)
        for index, pair in enumerate(chunk_copies):
            for copy in pair:
                copy.wait()
            if index == chunks - 1:
                rate[pl.ds(deepest, rows), :] = rate[pl.ds(deepest, rows), :] * open_sea
            carried = lax.fori_loop(index * chunk_segments, (index + 1) * chunk_segments, factor, carried)

        boundary = arrived(0)
        bottom = pl.ds(deepest, rows)
        last[pl.ds(0, rows), :] = solved[bottom, :] + (inverse[bottom, :] * rate[bottom, :]) * boundary
        sends += exchange(1)
        lax.fori_loop(0, levels // SEGMENT, back_first, boundary)
        lax.fori_loop(0, levels // SEGMENT, forward_second, (zeros, zeros))
        below = arrived(1)
        out_copies = []
        for index in reversed(range(chunks)):
            done = (chunks - 1 - index) * chunk_segments
            below = lax.fori_loop(done, done + chunk_segments, back_second, below)
            span = pl.ds(index * chunk, chunk)
            copy = pltpu.make_async_copy(state.at[span], out_hbm.at[0, span], out_sem.at[index])
            copy.start()
            out_copies.append(copy)
        for copy in sends:
            copy.wait_send()
        for copy in out_copies:
            copy.wait()

    @pl.when(is_ocean)
    def _():
        peers = [(sec, wrapped(column + shift - 1), 2 - shift) for sec in range(sections - 1) for shift in range(3)]
        program(LEV_OCN, TRC_OCN, peers, 1)

    @pl.when(jnp.logical_not(is_ocean))
    def _():
        peers = [(sections - 1, wrapped(column + shift - 1), section * 3 + 2 - shift) for shift in range(3)]
        program(LEV_ATM, TRC_ATM, peers, 2)


def shards(column_state, mixing, surface_mask, pairings, pairing_count, remap_weights):
    sections = lax.axis_size("sec")
    columns = lax.axis_size("col")
    _, rows_all, cells = column_state.shape
    blocks = surface_mask.shape[1]
    weight_rows = remap_weights.shape[1]
    kinds = weight_rows // cells
    rows_most = blocks * max(TRC_ATM, TRC_OCN)
    peers_most = 3 * (sections - 1)
    chunks_most = 5
    listing = jnp.transpose(pairings, (2, 0, 1))
    anywhere = pl.BlockSpec(memory_space=pl.ANY)
    column_buffer = pltpu.VMEM((rows_all, cells), jnp.float32)
    return pl.pallas_call(
        partial(kernel, sections, columns, blocks, kinds, cells),
        out_shape=jax.ShapeDtypeStruct(column_state.shape, jnp.float32),
        in_specs=[anywhere, anywhere, anywhere, anywhere, pl.BlockSpec(memory_space=pltpu.SMEM), anywhere],
        out_specs=anywhere,
        scratch_shapes=[
            column_buffer, column_buffer, column_buffer, column_buffer,
            pltpu.VMEM((weight_rows, cells), jnp.float32),
            pltpu.VMEM((weight_rows, 2 * cells), jnp.bfloat16),
            pltpu.VMEM((blocks, cells), jnp.int32),
            pltpu.VMEM(listing.shape, jnp.int32),
            pltpu.VMEM((rows_most, cells), jnp.float32),
            pltpu.VMEM((rows_most, cells), jnp.float32),
            pltpu.VMEM((2, peers_most, blocks, COUPLED * cells), jnp.float32),
            pltpu.VMEM((2, peers_most, blocks, COUPLED * cells), jnp.float32),
            pltpu.SemaphoreType.DMA((3 + WEIGHT_PARTS,)),
            pltpu.SemaphoreType.DMA((2, chunks_most)),
            pltpu.SemaphoreType.DMA((chunks_most,)),
            pltpu.SemaphoreType.DMA((2, peers_most)),
            pltpu.SemaphoreType.DMA((2, peers_most)),
        ],
        compiler_params=pltpu.CompilerParams(
            collective_id=0, has_side_effects=True, vmem_limit_bytes=62 * 1024 * 1024),
    )(column_state, mixing, surface_mask, listing, pairing_count, remap_weights)


def solution(mesh):
    placed = (
        P("sec", "col", None),
        P("sec", "col", None),
        P("sec", "col", None),
        P("sec", "col", None),
        P("sec", "col"),
        P("sec", "col", None),
    )
    return jax.shard_map(
        shards, mesh=mesh, in_specs=placed, out_specs=P("sec", "col", None), check_vma=False
    )
```

```python
import math
from functools import partial

import jax
import jax.numpy as jnp
from jax import lax
from jax.experimental import pallas as pl
from jax.experimental.pallas import tpu as pltpu
from jax.sharding import PartitionSpec as P

LEV_ATM = 128
LEV_OCN = 80
TRC_ATM = 5
TRC_OCN = 8
COUPLED = 4
SEGMENT = 16
WEIGHT_PARTS = 4
COMBINE_PERIODS = 2

MESH = pl.DeviceIdType.MESH


def split(values):
    high = values.astype(jnp.bfloat16)
    low = (values - high.astype(jnp.float32)).astype(jnp.bfloat16)
    return high, low


def reciprocal(values):
    first = pl.reciprocal(values, approx=True)
    return first * (2.0 - values * first)


def kernel(sections, columns, blocks, kinds, cells, state_hbm, mixing_hbm, mask_hbm, pairs_hbm, count_ref, weights_hbm,
           base_hbm, response_hbm, pattern_hbm, state, rate, inverse, upper, solved, pattern, weights, split_weights, mask, pairs, last, edge, send, recv,
           in_sem, chunk_sem, out_sem, send_sem, recv_sem):
    section = lax.axis_index("sec")
    column = lax.axis_index("col")
    is_ocean = section == sections - 1

    def wrapped(index):
        return lax.rem(index + columns, columns)

    def program(levels, tracers, peers, chunk_segments):
        rows = blocks * tracers
        deepest = (levels - 1) * rows
        chunk = chunk_segments * SEGMENT * rows
        chunks = levels // (chunk_segments * SEGMENT)

        barrier = pltpu.get_barrier_semaphore()
        for peer_sec, peer_col, _ in peers:
            pl.semaphore_signal(barrier, inc=1, device_id=(peer_sec, peer_col), device_id_type=MESH)

        mask_copy = pltpu.make_async_copy(mask_hbm.at[0], mask, in_sem.at[0])
        pairs_copy = pltpu.make_async_copy(pairs_hbm, pairs, in_sem.at[1])
        last_copy = pltpu.make_async_copy(
            state_hbm.at[0, pl.ds(deepest, rows)], last.at[pl.ds(0, rows)], in_sem.at[2])
        part = weights.shape[0] // WEIGHT_PARTS
        weights_copies = [
            pltpu.make_async_copy(
                weights_hbm.at[0, pl.ds(index * part, part)], weights.at[pl.ds(index * part, part)], in_sem.at[3 + index])
            for index in range(WEIGHT_PARTS)]
        first_copies = (mask_copy, pairs_copy, last_copy, *weights_copies)
        for copy in first_copies:
            copy.start()
        chunk_copies = []
        for index in range(chunks):
            span = pl.ds(index * chunk, chunk)
            chunk_copies.append((
                pltpu.make_async_copy(mixing_hbm.at[0, span], rate.at[span], chunk_sem.at[0, index]),
                pltpu.make_async_copy(state_hbm.at[0, span], state.at[span], chunk_sem.at[1, index]),
            ))
        for pair in chunk_copies:
            for copy in pair:
                copy.start()

        mask_copy.wait()
        pairs_copy.wait()
        list_length = pairs.shape[2]
        count_rows = -(-len(peers) * blocks // 16) * 16
        row = lax.broadcasted_iota(jnp.int32, (count_rows, 1), 0)
        wanted = jnp.full((count_rows, 1), -1, jnp.int32)
        for index, (peer_sec, peer_col, _) in enumerate(peers):
            first = (peer_sec * columns + peer_col) * blocks - index * blocks
            wanted = jnp.where((row >= index * blocks) & (row < (index + 1) * blocks), first + row, wanted)
        position = lax.broadcasted_iota(jnp.int32, (1, list_length), 1)
        target = jnp.where(position < count_ref[0, 0], pairs[1], -2)
        product = pairs[2] * blocks + pairs[0]
        to_rows = (target == wanted).astype(jnp.bfloat16)
        from_rows = (product == lax.broadcasted_iota(jnp.int32, (kinds * blocks, 1), 0)).astype(jnp.bfloat16)
        counts = lax.dot_general(
            to_rows, from_rows, (((1,), (1,)), ((), ())), preferred_element_type=jnp.float32).astype(jnp.bfloat16)
        counts_twice = jnp.concatenate([counts, counts], axis=1)
        sea = mask[...].astype(jnp.float32)

        edge[...] = jnp.zeros_like(edge)
        for field in range(tracers):
            edge[pl.ds(field, blocks, stride=tracers), :] = sea
        open_sea = edge[pl.ds(0, rows), :]
        edge[...] = jnp.zeros_like(edge)

        def exchange(step):
            surface = jnp.concatenate(
                [last[pl.ds(field, blocks, stride=tracers), :] * sea for field in range(COUPLED)], axis=0)
            surface_split = jnp.concatenate(split(surface), axis=0)
            half = COUPLED * blocks
            products = []
            for kind in range(kinds):
                span = pl.ds(kind * cells, cells)
                if step == 0:
                    if kind * WEIGHT_PARTS % kinds == 0:
                        weights_copies[kind * WEIGHT_PARTS // kinds].wait()
                    both = jnp.concatenate(split(weights[span, :]), axis=1)
                    split_weights[span, :] = both
                else:
                    both = split_weights[span, :]
                parts = jnp.dot(surface_split, both, preferred_element_type=jnp.float32)
                products.append(
                    (parts[:half, :cells] + parts[half:, :cells]) + (parts[:half, cells:] + parts[half:, cells:]))
            ordered = jnp.concatenate(
                [jnp.concatenate([item[field * blocks:(field + 1) * blocks] for item in products], axis=0)
                 for field in range(COUPLED)], axis=1)
            outgoing = jnp.dot(
                counts_twice, jnp.concatenate(split(ordered), axis=0), preferred_element_type=jnp.float32)
            copies = []
            for index, (peer_sec, peer_col, slot) in enumerate(peers):
                send[step, index] = outgoing[index * blocks:(index + 1) * blocks]
            if step == 0:
                pl.semaphore_wait(barrier, len(peers))
            for index, (peer_sec, peer_col, slot) in enumerate(peers):
                copy = pltpu.make_async_remote_copy(
                    src_ref=send.at[step, index], dst_ref=recv.at[step, slot],
                    send_sem=send_sem.at[step, index], recv_sem=recv_sem.at[step, slot],
                    device_id=(peer_sec, peer_col), device_id_type=MESH)
                copy.start()
                copies.append(copy)
            return copies

        def arrived(step):
            total = None
            for index, (peer_sec, peer_col, _) in enumerate(peers):
                pltpu.make_async_remote_copy(
                    src_ref=send.at[step, index], dst_ref=recv.at[step, index],
                    send_sem=send_sem.at[step, index], recv_sem=recv_sem.at[step, index],
                    device_id=(peer_sec, peer_col), device_id_type=MESH).wait_recv()
            for index in range(len(peers)):
                part = recv[step, index]
                total = part if total is None else total + part
            for field in range(COUPLED):
                edge[pl.ds(field, blocks, stride=tracers), :] = total[:, field * cells:(field + 1) * cells]
            return edge[pl.ds(0, rows), :]

        def at(level):
            return pl.ds(pl.multiple_of(level * rows, 8), rows)

        def factor(segment, carried):
            numer, value, above = carried
            denom = jnp.ones_like(numer)
            for offset in range(SEGMENT):
                here = at(segment * SEGMENT + offset)
                coupling = rate[here, :]
                next_denom = numer + coupling * denom
                numer = next_denom + coupling * numer
                scale = denom * reciprocal(next_denom)
                value = scale * state[here, :] + (scale * above) * value
                inverse[here, :] = scale
                upper[here, :] = scale * coupling
                solved[here, :] = value
                denom = next_denom
                above = coupling
            return numer * reciprocal(denom), value, above

        def back_first(index, below):
            segment = levels // SEGMENT - 1 - index
            for offset in reversed(range(SEGMENT)):
                here = at(segment * SEGMENT + offset)
                below = solved[here, :] + upper[here, :] * below
                solved[here, :] = below
            return below

        def forward_second(segment, carried):
            value, above = carried
            for offset in range(SEGMENT):
                here = at(segment * SEGMENT + offset)
                scale = inverse[here, :]
                coupling = rate[here, :]
                value = scale * solved[here, :] + (scale * above) * value
                solved[here, :] = value
                above = coupling
            return value, above

        def back_second(index, carried):
            segment = levels // SEGMENT - 1 - index
            below, response = carried
            for offset in reversed(range(SEGMENT)):
                here = at(segment * SEGMENT + offset)
                factor_here = upper[here, :]
                below = solved[here, :] + factor_here * below
                response = factor_here * response
                state[here, :] = below
                inverse[here, :] = response
            return below, response

        last_copy.wait()
        sends = exchange(0)

        zeros = jnp.zeros((rows, cells), jnp.float32)
        carried = (jnp.ones_like(zeros), zeros, zeros)
        for index, pair in enumerate(chunk_copies):
            for copy in pair:
                copy.wait()
            if index == chunks - 1:
                rate[pl.ds(deepest, rows), :] = rate[pl.ds(deepest, rows), :] * open_sea
            carried = lax.fori_loop(index * chunk_segments, (index + 1) * chunk_segments, factor, carried)

        boundary = arrived(0)
        bottom = pl.ds(deepest, rows)
        last[pl.ds(0, rows), :] = solved[bottom, :] + upper[bottom, :] * boundary
        sends += exchange(1)
        lax.fori_loop(0, levels // SEGMENT, back_first, boundary)
        lax.fori_loop(0, levels // SEGMENT, forward_second, (zeros, zeros))
        out_copies = []
        carried = (zeros, jnp.ones_like(zeros))
        for index in reversed(range(chunks)):
            done = (chunks - 1 - index) * chunk_segments
            carried = lax.fori_loop(done, done + chunk_segments, back_second, carried)
            span = pl.ds(index * chunk, chunk)
            for which, (source, target_hbm) in enumerate(((state, base_hbm), (inverse, response_hbm))):
                copy = pltpu.make_async_copy(source.at[span], target_hbm.at[span], out_sem.at[which, index])
                copy.start()
                out_copies.append(copy)
        boundary = arrived(1)
        pattern[...] = jnp.concatenate([boundary] * (pattern.shape[0] // rows), axis=0)
        pattern_copy = pltpu.make_async_copy(pattern, pattern_hbm, in_sem.at[0])
        pattern_copy.start()
        for copy in sends:
            copy.wait_send()
        for copy in out_copies:
            copy.wait()
        pattern_copy.wait()

    @pl.when(is_ocean)
    def _():
        peers = [(sec, wrapped(column + shift - 1), 2 - shift) for sec in range(sections - 1) for shift in range(3)]
        program(LEV_OCN, TRC_OCN, peers, 1)

    @pl.when(jnp.logical_not(is_ocean))
    def _():
        peers = [(sections - 1, wrapped(column + shift - 1), section * 3 + 2 - shift) for shift in range(3)]
        program(LEV_ATM, TRC_ATM, peers, 2)


def combine(base_hbm, response_hbm, pattern_hbm, out_hbm, base, response, pattern, result, in_sem, pattern_sem, out_sem):
    period = pattern.shape[0]
    chunk = COMBINE_PERIODS * period
    chunks = base.shape[0] // chunk
    pattern_copy = pltpu.make_async_copy(pattern_hbm, pattern, pattern_sem)
    pattern_copy.start()
    in_copies = []
    for index in range(chunks):
        span = pl.ds(index * chunk, chunk)
        in_copies.append((
            pltpu.make_async_copy(base_hbm.at[span], base.at[span], in_sem.at[0, index]),
            pltpu.make_async_copy(response_hbm.at[span], response.at[span], in_sem.at[1, index]),
        ))
        for copy in in_copies[-1]:
            copy.start()
    pattern_copy.wait()
    out_copies = []
    for index, pair in enumerate(in_copies):
        for copy in pair:
            copy.wait()
        for part in range(COMBINE_PERIODS):
            span = pl.ds(index * chunk + part * period, period)
            result[span, :] = base[span, :] + response[span, :] * pattern[...]
        span = pl.ds(index * chunk, chunk)
        copy = pltpu.make_async_copy(result.at[span], out_hbm.at[0, span], out_sem.at[index])
        copy.start()
        out_copies.append(copy)
    for copy in out_copies:
        copy.wait()


def shards(column_state, mixing, surface_mask, pairings, pairing_count, remap_weights):
    sections = lax.axis_size("sec")
    columns = lax.axis_size("col")
    _, rows_all, cells = column_state.shape
    blocks = surface_mask.shape[1]
    weight_rows = remap_weights.shape[1]
    kinds = weight_rows // cells
    rows_most = blocks * max(TRC_ATM, TRC_OCN)
    peers_most = 3 * (sections - 1)
    chunks_most = 5
    listing = jnp.transpose(pairings, (2, 0, 1))
    anywhere = pl.BlockSpec(memory_space=pl.ANY)
    column_buffer = pltpu.VMEM((rows_all, cells), jnp.float32)
    columns_shape = jax.ShapeDtypeStruct((rows_all, cells), jnp.float32)
    period = math.lcm(blocks * TRC_ATM, blocks * TRC_OCN)
    pattern_shape = jax.ShapeDtypeStruct((period, cells), jnp.float32)
    combine_chunks = rows_all // (COMBINE_PERIODS * period)
    base, response, pattern = pl.pallas_call(
        partial(kernel, sections, columns, blocks, kinds, cells),
        out_shape=(columns_shape, columns_shape, pattern_shape),
        in_specs=[anywhere, anywhere, anywhere, anywhere, pl.BlockSpec(memory_space=pltpu.SMEM), anywhere],
        out_specs=(anywhere, anywhere, anywhere),
        scratch_shapes=[
            column_buffer, column_buffer, column_buffer, column_buffer, column_buffer,
            pltpu.VMEM(pattern_shape.shape, jnp.float32),
            pltpu.VMEM((weight_rows, cells), jnp.float32),
            pltpu.VMEM((weight_rows, 2 * cells), jnp.bfloat16),
            pltpu.VMEM((blocks, cells), jnp.int32),
            pltpu.VMEM(listing.shape, jnp.int32),
            pltpu.VMEM((rows_most, cells), jnp.float32),
            pltpu.VMEM((rows_most, cells), jnp.float32),
            pltpu.VMEM((2, peers_most, blocks, COUPLED * cells), jnp.float32),
            pltpu.VMEM((2, peers_most, blocks, COUPLED * cells), jnp.float32),
            pltpu.SemaphoreType.DMA((3 + WEIGHT_PARTS,)),
            pltpu.SemaphoreType.DMA((2, chunks_most)),
            pltpu.SemaphoreType.DMA((2, chunks_most)),
            pltpu.SemaphoreType.DMA((2, peers_most)),
            pltpu.SemaphoreType.DMA((2, peers_most)),
        ],
        compiler_params=pltpu.CompilerParams(
            collective_id=0, has_side_effects=True, vmem_limit_bytes=62 * 1024 * 1024),
    )(column_state, mixing, surface_mask, listing, pairing_count, remap_weights)
    return pl.pallas_call(
        combine,
        out_shape=jax.ShapeDtypeStruct(column_state.shape, jnp.float32),
        in_specs=[anywhere, anywhere, anywhere],
        out_specs=anywhere,
        scratch_shapes=[
            column_buffer, column_buffer, pltpu.VMEM(pattern_shape.shape, jnp.float32), column_buffer,
            pltpu.SemaphoreType.DMA((2, combine_chunks)),
            pltpu.SemaphoreType.DMA,
            pltpu.SemaphoreType.DMA((combine_chunks,)),
        ],
        compiler_params=pltpu.CompilerParams(vmem_limit_bytes=62 * 1024 * 1024),
    )(base, response, pattern)


def solution(mesh):
    placed = (
        P("sec", "col", None),
        P("sec", "col", None),
        P("sec", "col", None),
        P("sec", "col", None),
        P("sec", "col"),
        P("sec", "col", None),
    )
    return jax.shard_map(
        shards, mesh=mesh, in_specs=placed, out_specs=P("sec", "col", None), check_vma=False
    )
```

```python
from functools import partial

import jax
import jax.numpy as jnp
from jax import lax
from jax.experimental import pallas as pl
from jax.experimental.pallas import tpu as pltpu
from jax.sharding import PartitionSpec as P

LEV_ATM = 128
LEV_OCN = 80
TRC_ATM = 5
TRC_OCN = 8
COUPLED = 4
SEGMENT = 16
WEIGHT_PARTS = 4
HAND_ON_CHUNKS = 8

MESH = pl.DeviceIdType.MESH


def split(values):
    high = values.astype(jnp.bfloat16)
    low = (values - high.astype(jnp.float32)).astype(jnp.bfloat16)
    return high, low


def reciprocal(values):
    first = pl.reciprocal(values, approx=True)
    return first * (2.0 - values * first)


def kernel(sections, columns, blocks, kinds, cells, state_hbm, mixing_hbm, mask_hbm, pairs_hbm, count_ref, weights_hbm,
           out_hbm, state, rate, inverse, upper, solved, weights, split_weights, mask, pairs, last, edge, send, recv,
           in_sem, chunk_sem, out_sem, send_sem, recv_sem):
    section = lax.axis_index("sec")
    column = lax.axis_index("col")
    is_ocean = section == sections - 1

    def wrapped(index):
        return lax.rem(index + columns, columns)

    def program(levels, tracers, peers, chunk_segments):
        rows = blocks * tracers
        deepest = (levels - 1) * rows
        chunk = chunk_segments * SEGMENT * rows
        chunks = levels // (chunk_segments * SEGMENT)

        barrier = pltpu.get_barrier_semaphore()
        for peer_sec, peer_col, _ in peers:
            pl.semaphore_signal(barrier, inc=1, device_id=(peer_sec, peer_col), device_id_type=MESH)

        mask_copy = pltpu.make_async_copy(mask_hbm.at[0], mask, in_sem.at[0])
        pairs_copy = pltpu.make_async_copy(pairs_hbm, pairs, in_sem.at[1])
        last_copy = pltpu.make_async_copy(
            state_hbm.at[0, pl.ds(deepest, rows)], last.at[pl.ds(0, rows)], in_sem.at[2])
        part = weights.shape[0] // WEIGHT_PARTS
        weights_copies = [
            pltpu.make_async_copy(
                weights_hbm.at[0, pl.ds(index * part, part)], weights.at[pl.ds(index * part, part)], in_sem.at[3 + index])
            for index in range(WEIGHT_PARTS)]
        first_copies = (mask_copy, pairs_copy, last_copy, *weights_copies)
        for copy in first_copies:
            copy.start()
        chunk_copies = []
        for index in range(chunks):
            span = pl.ds(index * chunk, chunk)
            chunk_copies.append((
                pltpu.make_async_copy(mixing_hbm.at[0, span], rate.at[span], chunk_sem.at[0, index]),
                pltpu.make_async_copy(state_hbm.at[0, span], state.at[span], chunk_sem.at[1, index]),
            ))

        def start_chunks(first, end):
            for pair in chunk_copies[first:end]:
                for copy in pair:
                    copy.start()

        start_chunks(0, 1)

        mask_copy.wait()
        pairs_copy.wait()
        list_length = pairs.shape[2]
        count_rows = -(-len(peers) * blocks // 16) * 16
        row = lax.broadcasted_iota(jnp.int32, (count_rows, 1), 0)
        wanted = jnp.full((count_rows, 1), -1, jnp.int32)
        for index, (peer_sec, peer_col, _) in enumerate(peers):
            first = (peer_sec * columns + peer_col) * blocks - index * blocks
            wanted = jnp.where((row >= index * blocks) & (row < (index + 1) * blocks), first + row, wanted)
        position = lax.broadcasted_iota(jnp.int32, (1, list_length), 1)
        target = jnp.where(position < count_ref[0, 0], pairs[1], -2)
        product = pairs[2] * blocks + pairs[0]
        to_rows = (target == wanted).astype(jnp.bfloat16)
        from_rows = (product == lax.broadcasted_iota(jnp.int32, (kinds * blocks, 1), 0)).astype(jnp.bfloat16)
        counts = lax.dot_general(
            to_rows, from_rows, (((1,), (1,)), ((), ())), preferred_element_type=jnp.float32).astype(jnp.bfloat16)
        counts_twice = jnp.concatenate([counts, counts], axis=1)
        sea = mask[...].astype(jnp.float32)

        edge[...] = jnp.zeros_like(edge)
        for field in range(tracers):
            edge[pl.ds(field, blocks, stride=tracers), :] = sea
        open_sea = edge[pl.ds(0, rows), :]
        edge[...] = jnp.zeros_like(edge)

        def exchange(step):
            surface = jnp.concatenate(
                [last[pl.ds(field, blocks, stride=tracers), :] * sea for field in range(COUPLED)], axis=0)
            surface_split = jnp.concatenate(split(surface), axis=0)
            half = COUPLED * blocks
            products = []
            for kind in range(kinds):
                span = pl.ds(kind * cells, cells)
                if step == 0:
                    if kind * WEIGHT_PARTS % kinds == 0:
                        part_index = kind * WEIGHT_PARTS // kinds
                        weights_copies[part_index].wait()
                        start_chunks(part_index + 1, part_index + 2 if part_index < WEIGHT_PARTS - 1 else chunks)
                    both = jnp.concatenate(split(weights[span, :]), axis=1)
                    split_weights[span, :] = both
                else:
                    both = split_weights[span, :]
                parts = jnp.dot(surface_split, both, preferred_element_type=jnp.float32)
                products.append(
                    (parts[:half, :cells] + parts[half:, :cells]) + (parts[:half, cells:] + parts[half:, cells:]))
            ordered = jnp.concatenate(
                [jnp.concatenate([item[field * blocks:(field + 1) * blocks] for item in products], axis=0)
                 for field in range(COUPLED)], axis=1)
            outgoing = jnp.dot(
                counts_twice, jnp.concatenate(split(ordered), axis=0), preferred_element_type=jnp.float32)
            copies = []
            for index, (peer_sec, peer_col, slot) in enumerate(peers):
                send[step, index] = outgoing[index * blocks:(index + 1) * blocks]
            if step == 0:
                pl.semaphore_wait(barrier, len(peers))
            for index, (peer_sec, peer_col, slot) in enumerate(peers):
                copy = pltpu.make_async_remote_copy(
                    src_ref=send.at[step, index], dst_ref=recv.at[step, slot],
                    send_sem=send_sem.at[step, index], recv_sem=recv_sem.at[step, slot],
                    device_id=(peer_sec, peer_col), device_id_type=MESH)
                copy.start()
                copies.append(copy)
            return copies

        def arrived(step):
            total = None
            for index, (peer_sec, peer_col, _) in enumerate(peers):
                pltpu.make_async_remote_copy(
                    src_ref=send.at[step, index], dst_ref=recv.at[step, index],
                    send_sem=send_sem.at[step, index], recv_sem=recv_sem.at[step, index],
                    device_id=(peer_sec, peer_col), device_id_type=MESH).wait_recv()
            for index in range(len(peers)):
                part = recv[step, index]
                total = part if total is None else total + part
            for field in range(COUPLED):
                edge[pl.ds(field, blocks, stride=tracers), :] = total[:, field * cells:(field + 1) * cells]
            return edge[pl.ds(0, rows), :]

        def at(level):
            return pl.ds(pl.multiple_of(level * rows, 8), rows)

        def factor(segment, carried):
            numer, value, above = carried
            denom = jnp.ones_like(numer)
            for offset in range(SEGMENT):
                here = at(segment * SEGMENT + offset)
                coupling = rate[here, :]
                next_denom = numer + coupling * denom
                numer = next_denom + coupling * numer
                scale = denom * reciprocal(next_denom)
                value = scale * state[here, :] + (scale * above) * value
                inverse[here, :] = scale
                upper[here, :] = scale * coupling
                solved[here, :] = value
                denom = next_denom
                above = coupling
            return numer * reciprocal(denom), value, above

        def back_first(index, below):
            segment = levels // SEGMENT - 1 - index
            for offset in reversed(range(SEGMENT)):
                here = at(segment * SEGMENT + offset)
                below = solved[here, :] + upper[here, :] * below
                solved[here, :] = below
            return below

        def forward_second(segment, carried):
            value, above = carried
            for offset in range(SEGMENT):
                here = at(segment * SEGMENT + offset)
                scale = inverse[here, :]
                coupling = rate[here, :]
                value = scale * solved[here, :] + (scale * above) * value
                solved[here, :] = value
                above = coupling
            return value, above

        def back_second(index, carried):
            segment = levels // SEGMENT - 1 - index
            below, response = carried
            for offset in reversed(range(SEGMENT)):
                here = at(segment * SEGMENT + offset)
                factor_here = upper[here, :]
                below = solved[here, :] + factor_here * below
                response = factor_here * response
                solved[here, :] = below
                upper[here, :] = response
            return below, response

        last_copy.wait()
        sends = exchange(0)

        zeros = jnp.zeros((rows, cells), jnp.float32)
        carried = (jnp.ones_like(zeros), zeros, zeros)
        for index, pair in enumerate(chunk_copies):
            for copy in pair:
                copy.wait()
            if index == chunks - 1:
                rate[pl.ds(deepest, rows), :] = rate[pl.ds(deepest, rows), :] * open_sea
            carried = lax.fori_loop(index * chunk_segments, (index + 1) * chunk_segments, factor, carried)

        boundary = arrived(0)
        bottom = pl.ds(deepest, rows)
        last[pl.ds(0, rows), :] = solved[bottom, :] + upper[bottom, :] * boundary
        sends += exchange(1)
        lax.fori_loop(0, levels // SEGMENT, back_first, boundary)
        lax.fori_loop(0, levels // SEGMENT, forward_second, (zeros, zeros))
        def join(segment, carried):
            for offset in range(SEGMENT):
                here = at(segment * SEGMENT + offset)
                state[here, :] = solved[here, :] + upper[here, :] * carried
            return carried

        lax.fori_loop(0, levels // SEGMENT, back_second, (zeros, jnp.ones_like(zeros)))
        boundary = arrived(1)
        out_copies = []
        for index in range(chunks):
            lax.fori_loop(index * chunk_segments, (index + 1) * chunk_segments, join, boundary)
            span = pl.ds(index * chunk, chunk)
            copy = pltpu.make_async_copy(state.at[span], out_hbm.at[0, span], out_sem.at[index])
            copy.start()
            out_copies.append(copy)
        for copy in sends:
            copy.wait_send()
        for copy in out_copies:
            copy.wait()

    @pl.when(is_ocean)
    def _():
        peers = [(sec, wrapped(column + shift - 1), 2 - shift) for sec in range(sections - 1) for shift in range(3)]
        program(LEV_OCN, TRC_OCN, peers, 1)

    @pl.when(jnp.logical_not(is_ocean))
    def _():
        peers = [(sections - 1, wrapped(column + shift - 1), section * 3 + 2 - shift) for shift in range(3)]
        program(LEV_ATM, TRC_ATM, peers, 2)


def hand_on(held_hbm, out_hbm, held, in_sem, out_sem):
    chunks = in_sem.shape[0]
    chunk = held.shape[0] // chunks
    spans = [pl.ds(index * chunk, chunk) for index in range(chunks)]
    in_copies = [
        pltpu.make_async_copy(held_hbm.at[0, span], held.at[span], in_sem.at[index]) for index, span in enumerate(spans)]
    out_copies = [
        pltpu.make_async_copy(held.at[span], out_hbm.at[0, span], out_sem.at[index]) for index, span in enumerate(spans)]
    for copy in in_copies:
        copy.start()
    for arriving, leaving in zip(in_copies, out_copies):
        arriving.wait()
        leaving.start()
    for copy in out_copies:
        copy.wait()


def shards(column_state, mixing, surface_mask, pairings, pairing_count, remap_weights):
    sections = lax.axis_size("sec")
    columns = lax.axis_size("col")
    _, rows_all, cells = column_state.shape
    blocks = surface_mask.shape[1]
    weight_rows = remap_weights.shape[1]
    kinds = weight_rows // cells
    rows_most = blocks * max(TRC_ATM, TRC_OCN)
    peers_most = 3 * (sections - 1)
    chunks_most = 5
    listing = jnp.transpose(pairings, (2, 0, 1))
    anywhere = pl.BlockSpec(memory_space=pl.ANY)
    column_buffer = pltpu.VMEM((rows_all, cells), jnp.float32)
    held = pl.pallas_call(
        partial(kernel, sections, columns, blocks, kinds, cells),
        out_shape=jax.ShapeDtypeStruct(column_state.shape, jnp.float32),
        in_specs=[anywhere, anywhere, anywhere, anywhere, pl.BlockSpec(memory_space=pltpu.SMEM), anywhere],
        out_specs=anywhere,
        scratch_shapes=[
            column_buffer, column_buffer, column_buffer, column_buffer, column_buffer,
            pltpu.VMEM((weight_rows, cells), jnp.float32),
            pltpu.VMEM((weight_rows, 2 * cells), jnp.bfloat16),
            pltpu.VMEM((blocks, cells), jnp.int32),
            pltpu.VMEM(listing.shape, jnp.int32),
            pltpu.VMEM((rows_most, cells), jnp.float32),
            pltpu.VMEM((rows_most, cells), jnp.float32),
            pltpu.VMEM((2, peers_most, blocks, COUPLED * cells), jnp.float32),
            pltpu.VMEM((2, peers_most, blocks, COUPLED * cells), jnp.float32),
            pltpu.SemaphoreType.DMA((3 + WEIGHT_PARTS,)),
            pltpu.SemaphoreType.DMA((2, chunks_most)),
            pltpu.SemaphoreType.DMA((chunks_most,)),
            pltpu.SemaphoreType.DMA((2, peers_most)),
            pltpu.SemaphoreType.DMA((2, peers_most)),
        ],
        compiler_params=pltpu.CompilerParams(
            collective_id=0, has_side_effects=True, vmem_limit_bytes=62 * 1024 * 1024),
    )(column_state, mixing, surface_mask, listing, pairing_count, remap_weights)
    return pl.pallas_call(
        hand_on,
        out_shape=jax.ShapeDtypeStruct(column_state.shape, jnp.float32),
        in_specs=[anywhere],
        out_specs=anywhere,
        scratch_shapes=[
            column_buffer,
            pltpu.SemaphoreType.DMA((HAND_ON_CHUNKS,)),
            pltpu.SemaphoreType.DMA((HAND_ON_CHUNKS,)),
        ],
        compiler_params=pltpu.CompilerParams(vmem_limit_bytes=62 * 1024 * 1024),
    )(held)

def solution(mesh):
    placed = (
        P("sec", "col", None),
        P("sec", "col", None),
        P("sec", "col", None),
        P("sec", "col", None),
        P("sec", "col"),
        P("sec", "col", None),
    )
    return jax.shard_map(
        shards, mesh=mesh, in_specs=placed, out_specs=P("sec", "col", None), check_vma=False
    )
```

```python
from functools import partial

import jax
import jax.numpy as jnp
from jax import lax
from jax.experimental import pallas as pl
from jax.experimental.pallas import tpu as pltpu
from jax.sharding import PartitionSpec as P

LEV_ATM = 128
LEV_OCN = 80
TRC_ATM = 5
TRC_OCN = 8
COUPLED = 4
SEGMENT = 16
WEIGHT_PARTS = 4
HAND_ON_CHUNKS = 8

MESH = pl.DeviceIdType.MESH


def split(values):
    high = values.astype(jnp.bfloat16)
    low = (values - high.astype(jnp.float32)).astype(jnp.bfloat16)
    return high, low


def reciprocal(values):
    first = pl.reciprocal(values, approx=True)
    return first * (2.0 - values * first)


def kernel(sections, columns, blocks, kinds, cells, state_hbm, mixing_hbm, mask_hbm, pairs_hbm, count_ref, weights_hbm,
           out_hbm, state, rate, inverse, upper, solved, weights, split_weights, mask, pairs, last, edge, send, recv,
           in_sem, chunk_sem, out_sem, send_sem, recv_sem):
    section = lax.axis_index("sec")
    column = lax.axis_index("col")
    is_ocean = section == sections - 1

    def wrapped(index):
        return lax.rem(index + columns, columns)

    def program(levels, tracers, peers, chunk_segments):
        rows = blocks * tracers
        deepest = (levels - 1) * rows
        chunk = chunk_segments * SEGMENT * rows
        chunks = levels // (chunk_segments * SEGMENT)

        barrier = pltpu.get_barrier_semaphore()
        for peer_sec, peer_col, _ in peers:
            pl.semaphore_signal(barrier, inc=1, device_id=(peer_sec, peer_col), device_id_type=MESH)

        mask_copy = pltpu.make_async_copy(mask_hbm.at[0], mask, in_sem.at[0])
        pairs_copy = pltpu.make_async_copy(pairs_hbm, pairs, in_sem.at[1])
        last_copy = pltpu.make_async_copy(
            state_hbm.at[0, pl.ds(deepest, rows)], last.at[pl.ds(0, rows)], in_sem.at[2])
        part = weights.shape[0] // WEIGHT_PARTS
        weights_copies = [
            pltpu.make_async_copy(
                weights_hbm.at[0, pl.ds(index * part, part)], weights.at[pl.ds(index * part, part)], in_sem.at[3 + index])
            for index in range(WEIGHT_PARTS)]
        first_copies = (mask_copy, pairs_copy, last_copy, *weights_copies)
        for copy in first_copies:
            copy.start()
        chunk_copies = []
        for index in range(chunks):
            span = pl.ds(index * chunk, chunk)
            chunk_copies.append((
                pltpu.make_async_copy(mixing_hbm.at[0, span], rate.at[span], chunk_sem.at[0, index]),
                pltpu.make_async_copy(state_hbm.at[0, span], state.at[span], chunk_sem.at[1, index]),
            ))

        def start_chunks(first, end):
            for pair in chunk_copies[first:end]:
                for copy in pair:
                    copy.start()

        start_chunks(0, 2)

        mask_copy.wait()
        pairs_copy.wait()
        list_length = pairs.shape[2]
        count_rows = -(-len(peers) * blocks // 16) * 16
        row = lax.broadcasted_iota(jnp.int32, (count_rows, 1), 0)
        wanted = jnp.full((count_rows, 1), -1, jnp.int32)
        for index, (peer_sec, peer_col, _) in enumerate(peers):
            first = (peer_sec * columns + peer_col) * blocks - index * blocks
            wanted = jnp.where((row >= index * blocks) & (row < (index + 1) * blocks), first + row, wanted)
        position = lax.broadcasted_iota(jnp.int32, (1, list_length), 1)
        target = jnp.where(position < count_ref[0, 0], pairs[1], -2)
        product = pairs[2] * blocks + pairs[0]
        to_rows = (target == wanted).astype(jnp.bfloat16)
        from_rows = (product == lax.broadcasted_iota(jnp.int32, (kinds * blocks, 1), 0)).astype(jnp.bfloat16)
        counts = lax.dot_general(
            to_rows, from_rows, (((1,), (1,)), ((), ())), preferred_element_type=jnp.float32).astype(jnp.bfloat16)
        counts_twice = jnp.concatenate([counts, counts], axis=1)
        sea = mask[...].astype(jnp.float32)

        edge[...] = jnp.zeros_like(edge)
        for field in range(tracers):
            edge[pl.ds(field, blocks, stride=tracers), :] = sea
        open_sea = edge[pl.ds(0, rows), :]
        edge[...] = jnp.zeros_like(edge)

        def exchange(step):
            surface = jnp.concatenate(
                [last[pl.ds(field, blocks, stride=tracers), :] * sea for field in range(COUPLED)], axis=0)
            surface_split = jnp.concatenate(split(surface), axis=0)
            half = COUPLED * blocks
            products = []
            for kind in range(kinds):
                span = pl.ds(kind * cells, cells)
                if step == 0:
                    if kind * WEIGHT_PARTS % kinds == 0:
                        part_index = kind * WEIGHT_PARTS // kinds
                        weights_copies[part_index].wait()
                        start_chunks(part_index + 2, part_index + 3 if part_index < WEIGHT_PARTS - 1 else chunks)
                    both = jnp.concatenate(split(weights[span, :]), axis=1)
                    split_weights[span, :] = both
                else:
                    both = split_weights[span, :]
                parts = jnp.dot(surface_split, both, preferred_element_type=jnp.float32)
                products.append(
                    (parts[:half, :cells] + parts[half:, :cells]) + (parts[:half, cells:] + parts[half:, cells:]))
            ordered = jnp.concatenate(
                [jnp.concatenate([item[field * blocks:(field + 1) * blocks] for item in products], axis=0)
                 for field in range(COUPLED)], axis=1)
            outgoing = jnp.dot(
                counts_twice, jnp.concatenate(split(ordered), axis=0), preferred_element_type=jnp.float32)
            copies = []
            for index, (peer_sec, peer_col, slot) in enumerate(peers):
                send[step, index] = outgoing[index * blocks:(index + 1) * blocks]
            if step == 0:
                pl.semaphore_wait(barrier, len(peers))
            for index, (peer_sec, peer_col, slot) in enumerate(peers):
                copy = pltpu.make_async_remote_copy(
                    src_ref=send.at[step, index], dst_ref=recv.at[step, slot],
                    send_sem=send_sem.at[step, index], recv_sem=recv_sem.at[step, slot],
                    device_id=(peer_sec, peer_col), device_id_type=MESH)
                copy.start()
                copies.append(copy)
            return copies

        def arrived(step):
            total = None
            for index, (peer_sec, peer_col, _) in enumerate(peers):
                pltpu.make_async_remote_copy(
                    src_ref=send.at[step, index], dst_ref=recv.at[step, index],
                    send_sem=send_sem.at[step, index], recv_sem=recv_sem.at[step, index],
                    device_id=(peer_sec, peer_col), device_id_type=MESH).wait_recv()
            for index in range(len(peers)):
                part = recv[step, index]
                total = part if total is None else total + part
            for field in range(COUPLED):
                edge[pl.ds(field, blocks, stride=tracers), :] = total[:, field * cells:(field + 1) * cells]
            return edge[pl.ds(0, rows), :]

        def at(level):
            return pl.ds(pl.multiple_of(level * rows, 8), rows)

        def factor(segment, carried):
            numer, value, above = carried
            denom = jnp.ones_like(numer)
            for offset in range(SEGMENT):
                here = at(segment * SEGMENT + offset)
                coupling = rate[here, :]
                next_denom = numer + coupling * denom
                numer = next_denom + coupling * numer
                scale = denom * reciprocal(next_denom)
                value = scale * state[here, :] + (scale * above) * value
                inverse[here, :] = scale
                upper[here, :] = scale * coupling
                solved[here, :] = value
                denom = next_denom
                above = coupling
            return numer * reciprocal(denom), value, above

        def back_first(index, below):
            segment = levels // SEGMENT - 1 - index
            for offset in reversed(range(SEGMENT)):
                here = at(segment * SEGMENT + offset)
                below = solved[here, :] + upper[here, :] * below
                solved[here, :] = below
            return below

        def forward_second(segment, carried):
            value, above = carried
            for offset in range(SEGMENT):
                here = at(segment * SEGMENT + offset)
                scale = inverse[here, :]
                coupling = rate[here, :]
                value = scale * solved[here, :] + (scale * above) * value
                solved[here, :] = value
                above = coupling
            return value, above

        def back_second(index, below):
            segment = levels // SEGMENT - 1 - index
            for offset in reversed(range(SEGMENT)):
                here = at(segment * SEGMENT + offset)
                below = solved[here, :] + upper[here, :] * below
                state[here, :] = below
            return below

        last_copy.wait()
        sends = exchange(0)

        zeros = jnp.zeros((rows, cells), jnp.float32)
        carried = (jnp.ones_like(zeros), zeros, zeros)
        for index, pair in enumerate(chunk_copies):
            for copy in pair:
                copy.wait()
            if index == chunks - 1:
                rate[pl.ds(deepest, rows), :] = rate[pl.ds(deepest, rows), :] * open_sea
            carried = lax.fori_loop(index * chunk_segments, (index + 1) * chunk_segments, factor, carried)

        boundary = arrived(0)
        bottom = pl.ds(deepest, rows)
        last[pl.ds(0, rows), :] = solved[bottom, :] + upper[bottom, :] * boundary
        sends += exchange(1)
        lax.fori_loop(0, levels // SEGMENT, back_first, boundary)
        lax.fori_loop(0, levels // SEGMENT, forward_second, (zeros, zeros))
        below = arrived(1)
        out_copies = []
        for index in reversed(range(chunks)):
            done = (chunks - 1 - index) * chunk_segments
            below = lax.fori_loop(done, done + chunk_segments, back_second, below)
            span = pl.ds(index * chunk, chunk)
            copy = pltpu.make_async_copy(state.at[span], out_hbm.at[0, span], out_sem.at[index])
            copy.start()
            out_copies.append(copy)
        for copy in sends:
            copy.wait_send()
        for copy in out_copies:
            copy.wait()

    @pl.when(is_ocean)
    def _():
        peers = [(sec, wrapped(column + shift - 1), 2 - shift) for sec in range(sections - 1) for shift in range(3)]
        program(LEV_OCN, TRC_OCN, peers, 1)

    @pl.when(jnp.logical_not(is_ocean))
    def _():
        peers = [(sections - 1, wrapped(column + shift - 1), section * 3 + 2 - shift) for shift in range(3)]
        program(LEV_ATM, TRC_ATM, peers, 2)


def hand_on(held_hbm, out_hbm, held, in_sem, out_sem):
    chunks = in_sem.shape[0]
    chunk = held.shape[0] // chunks
    spans = [pl.ds(index * chunk, chunk) for index in range(chunks)]
    in_copies = [
        pltpu.make_async_copy(held_hbm.at[0, span], held.at[span], in_sem.at[index]) for index, span in enumerate(spans)]
    out_copies = [
        pltpu.make_async_copy(held.at[span], out_hbm.at[0, span], out_sem.at[index]) for index, span in enumerate(spans)]
    for copy in in_copies:
        copy.start()
    for arriving, leaving in zip(in_copies, out_copies):
        arriving.wait()
        leaving.start()
    for copy in out_copies:
        copy.wait()


def shards(column_state, mixing, surface_mask, pairings, pairing_count, remap_weights):
    sections = lax.axis_size("sec")
    columns = lax.axis_size("col")
    _, rows_all, cells = column_state.shape
    blocks = surface_mask.shape[1]
    weight_rows = remap_weights.shape[1]
    kinds = weight_rows // cells
    rows_most = blocks * max(TRC_ATM, TRC_OCN)
    peers_most = 3 * (sections - 1)
    chunks_most = 5
    listing = jnp.transpose(pairings, (2, 0, 1))
    anywhere = pl.BlockSpec(memory_space=pl.ANY)
    column_buffer = pltpu.VMEM((rows_all, cells), jnp.float32)
    held = pl.pallas_call(
        partial(kernel, sections, columns, blocks, kinds, cells),
        out_shape=jax.ShapeDtypeStruct(column_state.shape, jnp.float32),
        in_specs=[anywhere, anywhere, anywhere, anywhere, pl.BlockSpec(memory_space=pltpu.SMEM), anywhere],
        out_specs=anywhere,
        scratch_shapes=[
            column_buffer, column_buffer, column_buffer, column_buffer, column_buffer,
            pltpu.VMEM((weight_rows, cells), jnp.float32),
            pltpu.VMEM((weight_rows, 2 * cells), jnp.bfloat16),
            pltpu.VMEM((blocks, cells), jnp.int32),
            pltpu.VMEM(listing.shape, jnp.int32),
            pltpu.VMEM((rows_most, cells), jnp.float32),
            pltpu.VMEM((rows_most, cells), jnp.float32),
            pltpu.VMEM((2, peers_most, blocks, COUPLED * cells), jnp.float32),
            pltpu.VMEM((2, peers_most, blocks, COUPLED * cells), jnp.float32),
            pltpu.SemaphoreType.DMA((3 + WEIGHT_PARTS,)),
            pltpu.SemaphoreType.DMA((2, chunks_most)),
            pltpu.SemaphoreType.DMA((chunks_most,)),
            pltpu.SemaphoreType.DMA((2, peers_most)),
            pltpu.SemaphoreType.DMA((2, peers_most)),
        ],
        compiler_params=pltpu.CompilerParams(
            collective_id=0, has_side_effects=True, vmem_limit_bytes=62 * 1024 * 1024),
    )(column_state, mixing, surface_mask, listing, pairing_count, remap_weights)
    return pl.pallas_call(
        hand_on,
        out_shape=jax.ShapeDtypeStruct(column_state.shape, jnp.float32),
        in_specs=[anywhere],
        out_specs=anywhere,
        scratch_shapes=[
            column_buffer,
            pltpu.SemaphoreType.DMA((HAND_ON_CHUNKS,)),
            pltpu.SemaphoreType.DMA((HAND_ON_CHUNKS,)),
        ],
        compiler_params=pltpu.CompilerParams(vmem_limit_bytes=62 * 1024 * 1024),
    )(held)

def solution(mesh):
    placed = (
        P("sec", "col", None),
        P("sec", "col", None),
        P("sec", "col", None),
        P("sec", "col", None),
        P("sec", "col"),
        P("sec", "col", None),
    )
    return jax.shard_map(
        shards, mesh=mesh, in_specs=placed, out_specs=P("sec", "col", None), check_vma=False
    )
```

```python
from functools import partial

import jax
import jax.numpy as jnp
from jax import lax
from jax.experimental import pallas as pl
from jax.experimental.pallas import tpu as pltpu
from jax.sharding import PartitionSpec as P

LEV_ATM = 128
LEV_OCN = 80
TRC_ATM = 5
TRC_OCN = 8
COUPLED = 4
SEGMENT = 16
WEIGHT_PARTS = 4
HAND_ON_CHUNKS = 8

MESH = pl.DeviceIdType.MESH


def split(values):
    high = values.astype(jnp.bfloat16)
    low = (values - high.astype(jnp.float32)).astype(jnp.bfloat16)
    return high, low


def reciprocal(values):
    first = pl.reciprocal(values, approx=True)
    return first * (2.0 - values * first)


def kernel(sections, columns, blocks, kinds, cells, state_hbm, mixing_hbm, mask_hbm, pairs_hbm, count_ref, weights_hbm,
           out_hbm, state, rate, inverse, upper, solved, weights, split_weights, mask, pairs, last, edge, send, recv,
           in_sem, chunk_sem, out_sem, send_sem, recv_sem):
    section = lax.axis_index("sec")
    column = lax.axis_index("col")
    is_ocean = section == sections - 1

    def wrapped(index):
        return lax.rem(index + columns, columns)

    def program(levels, tracers, peers, chunk_segments):
        rows = blocks * tracers
        deepest = (levels - 1) * rows
        chunk = chunk_segments * SEGMENT * rows
        chunks = levels // (chunk_segments * SEGMENT)

        barrier = pltpu.get_barrier_semaphore()
        for peer_sec, peer_col, _ in peers:
            pl.semaphore_signal(barrier, inc=1, device_id=(peer_sec, peer_col), device_id_type=MESH)

        mask_copy = pltpu.make_async_copy(mask_hbm.at[0], mask, in_sem.at[0])
        pairs_copy = pltpu.make_async_copy(pairs_hbm, pairs, in_sem.at[1])
        last_copy = pltpu.make_async_copy(
            state_hbm.at[0, pl.ds(deepest, rows)], last.at[pl.ds(0, rows)], in_sem.at[2])
        part = weights.shape[0] // WEIGHT_PARTS
        weights_copies = [
            pltpu.make_async_copy(
                weights_hbm.at[0, pl.ds(index * part, part)], weights.at[pl.ds(index * part, part)], in_sem.at[3 + index])
            for index in range(WEIGHT_PARTS)]
        first_copies = (mask_copy, pairs_copy, last_copy, *weights_copies)
        for copy in first_copies:
            copy.start()
        chunk_copies = []
        for index in range(chunks):
            span = pl.ds(index * chunk, chunk)
            chunk_copies.append((
                pltpu.make_async_copy(mixing_hbm.at[0, span], rate.at[span], chunk_sem.at[0, index]),
                pltpu.make_async_copy(state_hbm.at[0, span], state.at[span], chunk_sem.at[1, index]),
            ))

        def start_chunks(first, end):
            for pair in chunk_copies[first:end]:
                for copy in pair:
                    copy.start()

        start_chunks(0, 2)

        mask_copy.wait()
        pairs_copy.wait()
        list_length = pairs.shape[2]
        count_rows = -(-len(peers) * blocks // 16) * 16
        row = lax.broadcasted_iota(jnp.int32, (count_rows, 1), 0)
        wanted = jnp.full((count_rows, 1), -1, jnp.int32)
        for index, (peer_sec, peer_col, _) in enumerate(peers):
            first = (peer_sec * columns + peer_col) * blocks - index * blocks
            wanted = jnp.where((row >= index * blocks) & (row < (index + 1) * blocks), first + row, wanted)
        position = lax.broadcasted_iota(jnp.int32, (1, list_length), 1)
        target = jnp.where(position < count_ref[0, 0], pairs[1], -2)
        product = pairs[2] * blocks + pairs[0]
        to_rows = (target == wanted).astype(jnp.bfloat16)
        from_rows = (product == lax.broadcasted_iota(jnp.int32, (kinds * blocks, 1), 0)).astype(jnp.bfloat16)
        counts = lax.dot_general(
            to_rows, from_rows, (((1,), (1,)), ((), ())), preferred_element_type=jnp.float32).astype(jnp.bfloat16)
        counts_twice = jnp.concatenate([counts, counts], axis=1)
        sea = mask[...].astype(jnp.float32)

        edge[...] = jnp.zeros_like(edge)
        for field in range(tracers):
            edge[pl.ds(field, blocks, stride=tracers), :] = sea
        open_sea = edge[pl.ds(0, rows), :]
        edge[...] = jnp.zeros_like(edge)

        def exchange(step):
            surface = jnp.concatenate(
                [last[pl.ds(field, blocks, stride=tracers), :] * sea for field in range(COUPLED)], axis=0)
            surface_split = jnp.concatenate(split(surface), axis=0)
            half = COUPLED * blocks
            products = []
            for kind in range(kinds):
                span = pl.ds(kind * cells, cells)
                if step == 0:
                    if kind * WEIGHT_PARTS % kinds == 0:
                        part_index = kind * WEIGHT_PARTS // kinds
                        weights_copies[part_index].wait()
                        start_chunks(part_index + 2, part_index + 3 if part_index < WEIGHT_PARTS - 1 else chunks)
                    both = jnp.concatenate(split(weights[span, :]), axis=1)
                    split_weights[span, :] = both
                else:
                    both = split_weights[span, :]
                parts = jnp.dot(surface_split, both, preferred_element_type=jnp.float32)
                products.append(
                    (parts[:half, :cells] + parts[half:, :cells]) + (parts[:half, cells:] + parts[half:, cells:]))
            ordered = jnp.concatenate(
                [jnp.concatenate([item[field * blocks:(field + 1) * blocks] for item in products], axis=0)
                 for field in range(COUPLED)], axis=1)
            outgoing = jnp.dot(
                counts_twice, jnp.concatenate(split(ordered), axis=0), preferred_element_type=jnp.float32)
            copies = []
            for index, (peer_sec, peer_col, slot) in enumerate(peers):
                send[step, index] = outgoing[index * blocks:(index + 1) * blocks]
            if step == 0:
                pl.semaphore_wait(barrier, len(peers))
            for index, (peer_sec, peer_col, slot) in enumerate(peers):
                copy = pltpu.make_async_remote_copy(
                    src_ref=send.at[step, index], dst_ref=recv.at[step, slot],
                    send_sem=send_sem.at[step, index], recv_sem=recv_sem.at[step, slot],
                    device_id=(peer_sec, peer_col), device_id_type=MESH)
                copy.start()
                copies.append(copy)
            return copies

        def arrived(step):
            total = None
            for index, (peer_sec, peer_col, _) in enumerate(peers):
                pltpu.make_async_remote_copy(
                    src_ref=send.at[step, index], dst_ref=recv.at[step, index],
                    send_sem=send_sem.at[step, index], recv_sem=recv_sem.at[step, index],
                    device_id=(peer_sec, peer_col), device_id_type=MESH).wait_recv()
            for index in range(len(peers)):
                part = recv[step, index]
                total = part if total is None else total + part
            for field in range(COUPLED):
                edge[pl.ds(field, blocks, stride=tracers), :] = total[:, field * cells:(field + 1) * cells]
            return edge[pl.ds(0, rows), :]

        def at(level):
            return pl.ds(pl.multiple_of(level * rows, 8), rows)

        def factor(segment, carried):
            numer, value, above = carried
            denom = jnp.ones_like(numer)
            for offset in range(SEGMENT):
                here = at(segment * SEGMENT + offset)
                coupling = rate[here, :]
                next_denom = numer + coupling * denom
                numer = next_denom + coupling * numer
                scale = denom * reciprocal(next_denom)
                value = scale * state[here, :] + (scale * above) * value
                inverse[here, :] = scale
                upper[here, :] = scale * coupling
                solved[here, :] = value
                denom = next_denom
                above = coupling
            return numer * reciprocal(denom), value, above

        def back_first(index, below):
            segment = levels // SEGMENT - 1 - index
            for offset in reversed(range(SEGMENT)):
                here = at(segment * SEGMENT + offset)
                below = solved[here, :] + upper[here, :] * below
                solved[here, :] = below
            return below

        def forward_second(segment, carried):
            value, above = carried
            for offset in range(SEGMENT):
                here = at(segment * SEGMENT + offset)
                scale = inverse[here, :]
                coupling = rate[here, :]
                value = scale * solved[here, :] + (scale * above) * value
                solved[here, :] = value
                above = coupling
            return value, above

        def back_second(index, below):
            segment = levels // SEGMENT - 1 - index
            for offset in reversed(range(SEGMENT)):
                here = at(segment * SEGMENT + offset)
                below = solved[here, :] + upper[here, :] * below
                state[here, :] = below
            return below

        last_copy.wait()
        sends = exchange(0)

        zeros = jnp.zeros((rows, cells), jnp.float32)
        carried = (jnp.ones_like(zeros), zeros, zeros)
        for index, pair in enumerate(chunk_copies):
            for copy in pair:
                copy.wait()
            if index == chunks - 1:
                rate[pl.ds(deepest, rows), :] = rate[pl.ds(deepest, rows), :] * open_sea
            carried = lax.fori_loop(index * chunk_segments, (index + 1) * chunk_segments, factor, carried)

        boundary = arrived(0)
        bottom = pl.ds(deepest, rows)
        last[pl.ds(0, rows), :] = solved[bottom, :] + upper[bottom, :] * boundary
        sends += exchange(1)
        lax.fori_loop(0, levels // SEGMENT, back_first, boundary)
        lax.fori_loop(0, levels // SEGMENT, forward_second, (zeros, zeros))
        below = arrived(1)
        out_copies = []
        half = SEGMENT * rows // 2
        for index in reversed(range(levels // SEGMENT)):
            below = back_second(levels // SEGMENT - 1 - index, below)
            for side in (1, 0):
                span = pl.ds((2 * index + side) * half, half)
                copy = pltpu.make_async_copy(state.at[span], out_hbm.at[0, span], out_sem.at[2 * index + side])
                copy.start()
                out_copies.append(copy)
        for copy in sends:
            copy.wait_send()
        for copy in out_copies:
            copy.wait()

    @pl.when(is_ocean)
    def _():
        peers = [(sec, wrapped(column + shift - 1), 2 - shift) for sec in range(sections - 1) for shift in range(3)]
        program(LEV_OCN, TRC_OCN, peers, 1)

    @pl.when(jnp.logical_not(is_ocean))
    def _():
        peers = [(sections - 1, wrapped(column + shift - 1), section * 3 + 2 - shift) for shift in range(3)]
        program(LEV_ATM, TRC_ATM, peers, 2)


def hand_on(held_hbm, out_hbm, held, in_sem, out_sem):
    chunks = in_sem.shape[0]
    chunk = held.shape[0] // chunks
    spans = [pl.ds(index * chunk, chunk) for index in range(chunks)]
    in_copies = [
        pltpu.make_async_copy(held_hbm.at[0, span], held.at[span], in_sem.at[index]) for index, span in enumerate(spans)]
    out_copies = [
        pltpu.make_async_copy(held.at[span], out_hbm.at[0, span], out_sem.at[index]) for index, span in enumerate(spans)]
    for copy in in_copies:
        copy.start()
    for arriving, leaving in zip(in_copies, out_copies):
        arriving.wait()
        leaving.start()
    for copy in out_copies:
        copy.wait()


def shards(column_state, mixing, surface_mask, pairings, pairing_count, remap_weights):
    sections = lax.axis_size("sec")
    columns = lax.axis_size("col")
    _, rows_all, cells = column_state.shape
    blocks = surface_mask.shape[1]
    weight_rows = remap_weights.shape[1]
    kinds = weight_rows // cells
    rows_most = blocks * max(TRC_ATM, TRC_OCN)
    peers_most = 3 * (sections - 1)
    chunks_most = 5
    listing = jnp.transpose(pairings, (2, 0, 1))
    anywhere = pl.BlockSpec(memory_space=pl.ANY)
    column_buffer = pltpu.VMEM((rows_all, cells), jnp.float32)
    held = pl.pallas_call(
        partial(kernel, sections, columns, blocks, kinds, cells),
        out_shape=jax.ShapeDtypeStruct(column_state.shape, jnp.float32),
        in_specs=[anywhere, anywhere, anywhere, anywhere, pl.BlockSpec(memory_space=pltpu.SMEM), anywhere],
        out_specs=anywhere,
        scratch_shapes=[
            column_buffer, column_buffer, column_buffer, column_buffer, column_buffer,
            pltpu.VMEM((weight_rows, cells), jnp.float32),
            pltpu.VMEM((weight_rows, 2 * cells), jnp.bfloat16),
            pltpu.VMEM((blocks, cells), jnp.int32),
            pltpu.VMEM(listing.shape, jnp.int32),
            pltpu.VMEM((rows_most, cells), jnp.float32),
            pltpu.VMEM((rows_most, cells), jnp.float32),
            pltpu.VMEM((2, peers_most, blocks, COUPLED * cells), jnp.float32),
            pltpu.VMEM((2, peers_most, blocks, COUPLED * cells), jnp.float32),
            pltpu.SemaphoreType.DMA((3 + WEIGHT_PARTS,)),
            pltpu.SemaphoreType.DMA((2, chunks_most)),
            pltpu.SemaphoreType.DMA((2 * max(LEV_ATM, LEV_OCN) // SEGMENT,)),
            pltpu.SemaphoreType.DMA((2, peers_most)),
            pltpu.SemaphoreType.DMA((2, peers_most)),
        ],
        compiler_params=pltpu.CompilerParams(
            collective_id=0, has_side_effects=True, vmem_limit_bytes=62 * 1024 * 1024),
    )(column_state, mixing, surface_mask, listing, pairing_count, remap_weights)
    return pl.pallas_call(
        hand_on,
        out_shape=jax.ShapeDtypeStruct(column_state.shape, jnp.float32),
        in_specs=[anywhere],
        out_specs=anywhere,
        scratch_shapes=[
            column_buffer,
            pltpu.SemaphoreType.DMA((HAND_ON_CHUNKS,)),
            pltpu.SemaphoreType.DMA((HAND_ON_CHUNKS,)),
        ],
        compiler_params=pltpu.CompilerParams(vmem_limit_bytes=62 * 1024 * 1024),
    )(held)

def solution(mesh):
    placed = (
        P("sec", "col", None),
        P("sec", "col", None),
        P("sec", "col", None),
        P("sec", "col", None),
        P("sec", "col"),
        P("sec", "col", None),
    )
    return jax.shard_map(
        shards, mesh=mesh, in_specs=placed, out_specs=P("sec", "col", None), check_vma=False
    )
```

```python
from functools import partial

import jax
import jax.numpy as jnp
from jax import lax
from jax.experimental import pallas as pl
from jax.experimental.pallas import tpu as pltpu
from jax.sharding import PartitionSpec as P

LEV_ATM = 128
LEV_OCN = 80
TRC_ATM = 5
TRC_OCN = 8
COUPLED = 4
SEGMENT = 16
WEIGHT_PARTS = 4
HAND_ON_CHUNKS = 8

MESH = pl.DeviceIdType.MESH


def split(values):
    high = values.astype(jnp.bfloat16)
    low = (values - high.astype(jnp.float32)).astype(jnp.bfloat16)
    return high, low


def reciprocal(values):
    first = pl.reciprocal(values, approx=True)
    return first * (2.0 - values * first)


def kernel(sections, columns, blocks, kinds, cells, state_hbm, mixing_hbm, mask_hbm, pairs_hbm, count_ref, weights_hbm,
           out_hbm, state, rate, inverse, upper, solved, weights, split_weights, mask, pairs, last, edge, send, recv,
           in_sem, chunk_sem, out_sem, send_sem, recv_sem):
    section = lax.axis_index("sec")
    column = lax.axis_index("col")
    is_ocean = section == sections - 1

    def wrapped(index):
        return lax.rem(index + columns, columns)

    def program(levels, tracers, peers, chunk_segments):
        rows = blocks * tracers
        deepest = (levels - 1) * rows
        chunk = chunk_segments * SEGMENT * rows
        chunks = levels // (chunk_segments * SEGMENT)

        barrier = pltpu.get_barrier_semaphore()
        for peer_sec, peer_col, _ in peers:
            pl.semaphore_signal(barrier, inc=1, device_id=(peer_sec, peer_col), device_id_type=MESH)

        mask_copy = pltpu.make_async_copy(mask_hbm.at[0], mask, in_sem.at[0])
        pairs_copy = pltpu.make_async_copy(pairs_hbm, pairs, in_sem.at[1])
        last_copy = pltpu.make_async_copy(
            state_hbm.at[0, pl.ds(deepest, rows)], last.at[pl.ds(0, rows)], in_sem.at[2])
        part = weights.shape[0] // WEIGHT_PARTS
        weights_copies = [
            pltpu.make_async_copy(
                weights_hbm.at[0, pl.ds(index * part, part)], weights.at[pl.ds(index * part, part)], in_sem.at[3 + index])
            for index in range(WEIGHT_PARTS)]
        first_copies = (mask_copy, pairs_copy, last_copy, *weights_copies)
        for copy in first_copies:
            copy.start()
        chunk_copies = []
        for index in range(chunks):
            span = pl.ds(index * chunk, chunk)
            chunk_copies.append((
                pltpu.make_async_copy(mixing_hbm.at[0, span], rate.at[span], chunk_sem.at[0, index]),
                pltpu.make_async_copy(state_hbm.at[0, span], state.at[span], chunk_sem.at[1, index]),
            ))

        def start_chunks(first, end):
            for pair in chunk_copies[first:end]:
                for copy in pair:
                    copy.start()

        start_chunks(0, 2)

        mask_copy.wait()
        pairs_copy.wait()
        list_length = pairs.shape[2]
        count_rows = -(-len(peers) * blocks // 16) * 16
        row = lax.broadcasted_iota(jnp.int32, (count_rows, 1), 0)
        wanted = jnp.full((count_rows, 1), -1, jnp.int32)
        for index, (peer_sec, peer_col, _) in enumerate(peers):
            first = (peer_sec * columns + peer_col) * blocks - index * blocks
            wanted = jnp.where((row >= index * blocks) & (row < (index + 1) * blocks), first + row, wanted)
        position = lax.broadcasted_iota(jnp.int32, (1, list_length), 1)
        target = jnp.where(position < count_ref[0, 0], pairs[1], -2)
        product = pairs[2] * blocks + pairs[0]
        to_rows = (target == wanted).astype(jnp.bfloat16)
        from_rows = (product == lax.broadcasted_iota(jnp.int32, (kinds * blocks, 1), 0)).astype(jnp.bfloat16)
        counts = lax.dot_general(
            to_rows, from_rows, (((1,), (1,)), ((), ())), preferred_element_type=jnp.float32).astype(jnp.bfloat16)
        counts_twice = jnp.concatenate([counts, counts], axis=1)
        sea = mask[...].astype(jnp.float32)

        edge[...] = jnp.zeros_like(edge)
        for field in range(tracers):
            edge[pl.ds(field, blocks, stride=tracers), :] = sea
        open_sea = edge[pl.ds(0, rows), :]
        edge[...] = jnp.zeros_like(edge)

        def exchange(step):
            surface = jnp.concatenate(
                [last[pl.ds(field, blocks, stride=tracers), :] * sea for field in range(COUPLED)], axis=0)
            surface_split = jnp.concatenate(split(surface), axis=0)
            half = COUPLED * blocks
            products = []
            for kind in range(kinds):
                span = pl.ds(kind * cells, cells)
                if step == 0:
                    if kind * WEIGHT_PARTS % kinds == 0:
                        part_index = kind * WEIGHT_PARTS // kinds
                        weights_copies[part_index].wait()
                        start_chunks(part_index + 2, part_index + 3 if part_index < WEIGHT_PARTS - 1 else chunks)
                    both = jnp.concatenate(split(weights[span, :]), axis=1)
                    split_weights[span, :] = both
                else:
                    both = split_weights[span, :]
                parts = jnp.dot(surface_split, both, preferred_element_type=jnp.float32)
                products.append(
                    (parts[:half, :cells] + parts[half:, :cells]) + (parts[:half, cells:] + parts[half:, cells:]))
            ordered = jnp.concatenate(
                [jnp.concatenate([item[field * blocks:(field + 1) * blocks] for item in products], axis=0)
                 for field in range(COUPLED)], axis=1)
            outgoing = jnp.dot(
                counts_twice, jnp.concatenate(split(ordered), axis=0), preferred_element_type=jnp.float32)
            copies = []
            for index, (peer_sec, peer_col, slot) in enumerate(peers):
                send[step, index] = outgoing[index * blocks:(index + 1) * blocks]
            if step == 0:
                pl.semaphore_wait(barrier, len(peers))
            for index, (peer_sec, peer_col, slot) in enumerate(peers):
                copy = pltpu.make_async_remote_copy(
                    src_ref=send.at[step, index], dst_ref=recv.at[step, slot],
                    send_sem=send_sem.at[step, index], recv_sem=recv_sem.at[step, slot],
                    device_id=(peer_sec, peer_col), device_id_type=MESH)
                copy.start()
                copies.append(copy)
            return copies

        def arrived(step):
            total = None
            for index, (peer_sec, peer_col, _) in enumerate(peers):
                pltpu.make_async_remote_copy(
                    src_ref=send.at[step, index], dst_ref=recv.at[step, index],
                    send_sem=send_sem.at[step, index], recv_sem=recv_sem.at[step, index],
                    device_id=(peer_sec, peer_col), device_id_type=MESH).wait_recv()
            for index in range(len(peers)):
                part = recv[step, index]
                total = part if total is None else total + part
            for field in range(COUPLED):
                edge[pl.ds(field, blocks, stride=tracers), :] = total[:, field * cells:(field + 1) * cells]
            return edge[pl.ds(0, rows), :]

        def at(level):
            return pl.ds(pl.multiple_of(level * rows, 8), rows)

        def factor(segment, carried):
            numer, value, above = carried
            denom = jnp.ones_like(numer)
            for offset in range(SEGMENT):
                here = at(segment * SEGMENT + offset)
                coupling = rate[here, :]
                next_denom = numer + coupling * denom
                numer = next_denom + coupling * numer
                scale = denom * reciprocal(next_denom)
                value = scale * state[here, :] + (scale * above) * value
                inverse[here, :] = scale
                upper[here, :] = scale * coupling
                solved[here, :] = value
                denom = next_denom
                above = coupling
            return numer * reciprocal(denom), value, above

        def back_first(index, below):
            segment = levels // SEGMENT - 1 - index
            for offset in reversed(range(SEGMENT)):
                here = at(segment * SEGMENT + offset)
                below = solved[here, :] + upper[here, :] * below
                solved[here, :] = below
            return below

        def forward_second(segment, carried):
            value, above = carried
            for offset in range(SEGMENT):
                here = at(segment * SEGMENT + offset)
                scale = inverse[here, :]
                coupling = rate[here, :]
                value = scale * solved[here, :] + (scale * above) * value
                solved[here, :] = value
                above = coupling
            return value, above

        def back_second(index, below):
            segment = levels // SEGMENT - 1 - index
            for offset in reversed(range(SEGMENT)):
                here = at(segment * SEGMENT + offset)
                below = solved[here, :] + upper[here, :] * below
                state[here, :] = below
            return below

        last_copy.wait()
        sends = exchange(0)

        zeros = jnp.zeros((rows, cells), jnp.float32)
        carried = (jnp.ones_like(zeros), zeros, zeros)
        for index, pair in enumerate(chunk_copies):
            for copy in pair:
                copy.wait()
            if index == chunks - 1:
                rate[pl.ds(deepest, rows), :] = rate[pl.ds(deepest, rows), :] * open_sea
            carried = lax.fori_loop(index * chunk_segments, (index + 1) * chunk_segments, factor, carried)

        boundary = arrived(0)
        bottom = pl.ds(deepest, rows)
        last[pl.ds(0, rows), :] = solved[bottom, :] + upper[bottom, :] * boundary
        sends += exchange(1)
        lax.fori_loop(0, levels // SEGMENT, back_first, boundary)
        lax.fori_loop(0, levels // SEGMENT, forward_second, (zeros, zeros))
        below = arrived(1)
        out_copies = []
        for index in reversed(range(chunks)):
            done = (chunks - 1 - index) * chunk_segments
            below = lax.fori_loop(done, done + chunk_segments, back_second, below)
            span = pl.ds(index * chunk, chunk)
            copy = pltpu.make_async_copy(state.at[span], out_hbm.at[0, span], out_sem.at[index])
            copy.start()
            out_copies.append(copy)
        for copy in sends:
            copy.wait_send()
        for copy in out_copies:
            copy.wait()

    @pl.when(is_ocean)
    def _():
        peers = [(sec, wrapped(column + shift - 1), 2 - shift) for sec in range(sections - 1) for shift in range(3)]
        program(LEV_OCN, TRC_OCN, peers, 1)

    @pl.when(jnp.logical_not(is_ocean))
    def _():
        peers = [(sections - 1, wrapped(column + shift - 1), section * 3 + 2 - shift) for shift in range(3)]
        program(LEV_ATM, TRC_ATM, peers, 2)


def hand_on(held_hbm, out_hbm, sem):
    chunks = sem.shape[0]
    chunk = held_hbm.shape[1] // chunks
    copies = []
    for index in range(chunks):
        span = pl.ds(index * chunk, chunk)
        copies.append(pltpu.make_async_copy(held_hbm.at[0, span], out_hbm.at[0, span], sem.at[index]))
        copies[-1].start()
    for copy in copies:
        copy.wait()


def shards(column_state, mixing, surface_mask, pairings, pairing_count, remap_weights):
    sections = lax.axis_size("sec")
    columns = lax.axis_size("col")
    _, rows_all, cells = column_state.shape
    blocks = surface_mask.shape[1]
    weight_rows = remap_weights.shape[1]
    kinds = weight_rows // cells
    rows_most = blocks * max(TRC_ATM, TRC_OCN)
    peers_most = 3 * (sections - 1)
    chunks_most = 5
    listing = jnp.transpose(pairings, (2, 0, 1))
    anywhere = pl.BlockSpec(memory_space=pl.ANY)
    column_buffer = pltpu.VMEM((rows_all, cells), jnp.float32)
    held = pl.pallas_call(
        partial(kernel, sections, columns, blocks, kinds, cells),
        out_shape=jax.ShapeDtypeStruct(column_state.shape, jnp.float32),
        in_specs=[anywhere, anywhere, anywhere, anywhere, pl.BlockSpec(memory_space=pltpu.SMEM), anywhere],
        out_specs=anywhere,
        scratch_shapes=[
            column_buffer, column_buffer, column_buffer, column_buffer, column_buffer,
            pltpu.VMEM((weight_rows, cells), jnp.float32),
            pltpu.VMEM((weight_rows, 2 * cells), jnp.bfloat16),
            pltpu.VMEM((blocks, cells), jnp.int32),
            pltpu.VMEM(listing.shape, jnp.int32),
            pltpu.VMEM((rows_most, cells), jnp.float32),
            pltpu.VMEM((rows_most, cells), jnp.float32),
            pltpu.VMEM((2, peers_most, blocks, COUPLED * cells), jnp.float32),
            pltpu.VMEM((2, peers_most, blocks, COUPLED * cells), jnp.float32),
            pltpu.SemaphoreType.DMA((3 + WEIGHT_PARTS,)),
            pltpu.SemaphoreType.DMA((2, chunks_most)),
            pltpu.SemaphoreType.DMA((chunks_most,)),
            pltpu.SemaphoreType.DMA((2, peers_most)),
            pltpu.SemaphoreType.DMA((2, peers_most)),
        ],
        compiler_params=pltpu.CompilerParams(
            collective_id=0, has_side_effects=True, vmem_limit_bytes=62 * 1024 * 1024),
    )(column_state, mixing, surface_mask, listing, pairing_count, remap_weights)
    return pl.pallas_call(
        hand_on,
        out_shape=jax.ShapeDtypeStruct(column_state.shape, jnp.float32),
        in_specs=[anywhere],
        out_specs=anywhere,
        scratch_shapes=[
            pltpu.SemaphoreType.DMA((HAND_ON_CHUNKS,)),
        ],
        compiler_params=pltpu.CompilerParams(vmem_limit_bytes=62 * 1024 * 1024),
    )(held)

def solution(mesh):
    placed = (
        P("sec", "col", None),
        P("sec", "col", None),
        P("sec", "col", None),
        P("sec", "col", None),
        P("sec", "col"),
        P("sec", "col", None),
    )
    return jax.shard_map(
        shards, mesh=mesh, in_specs=placed, out_specs=P("sec", "col", None), check_vma=False
    )
```
